32 devices in a mesh: grp: 2 (over y), lat: 4 (over z), tm: 2 (over x), chan: 2 (over core).
Axes of the slice: x: 2, y: 2, z: 4, core: 2. Of those that a mesh axis runs over, the one named last changes fastest.
Arguments:
- innovations: bfloat16 [4, 4, 73, 32, 128], P(None, ('grp', 'tm'), None, ('lat', 'chan')), parts along dimension 1, may hold values from -6 to 6
- obs_mask: int32 [4, 8, 4], P(('grp', 'tm'), ('lat', 'chan')), parts along dimension 0, may hold values 0 or 1
- slopes: bfloat16 [4, 128, 32, 128], P(('grp', 'tm'), 'chan', 'lat'), parts along dimension 0, may hold values from -0.14941406 to 1.09375
- layer_of: int32 [2], replicated, may hold values from 0 to 7
- weight_in: bfloat16 [8, 3, 3, 73, 128], P(None, None, None, None, 'chan'), may hold values from -0.1875 to 0.1875
- weight_out: bfloat16 [8, 3, 3, 128, 73], P(None, None, None, 'chan'), may hold values from -0.25 to 0.25
Outputs:
- gradients: float32 [4, 4, 73, 32, 128], P(None, ('grp', 'tm'), None, ('lat', 'chan')), parts along dimension 1
The draws below stay inside these ranges and needn't reach their ends.
There are 2 independent parts, one for each index of `grp`. The reference program is written for one: setup_inputs(seed, part) draws one part's arguments, and reference() takes and returns one part's arrays. A program takes and returns all parts, laid end to end along the dimension named above; an argument that names none is the same for every part. Nothing has to cross between parts.
All inputs are finite; a program needn't handle non-finite values. No bound on the sum of `obs_mask` on one device may be relied on, other than what follows from the above.
Results may differ from the reference program's by a relative error of at most 0.011.
Values may be sent and summed in bfloat16 or wider, within the bound.
No kernel may reach another device: no remote copies, remote signals or barrier semaphores. Data moves between devices by JAX's collectives and lax.ppermute only.
A program may use at most 64 MiB of HBM per device.

```python
import jax
import jax.numpy as jnp
from jax import lax

C = 73
HID = 128
LAYERS = 8
FRONTS = 4
WIN = 128
SECTIONS = 2
LATS = 32


def set_ends(drawn, stream_key, low, largest):
    longest = drawn.shape.index(max(drawn.shape))
    spots = []
    for shift in (0, 1):
        where = [jax.random.randint(jax.random.fold_in(stream_key, axis), (), 0, length) for axis, length in enumerate(drawn.shape)]
        where[longest] = (where[longest] + shift) % drawn.shape[longest]
        spots.append(tuple(where))
    return drawn.at[spots[0]].set(low).at[spots[1]].set(largest)


def shard_levels(stream_key, shape, shards, smallest, largest):
    factor_of = 1.0
    for dim, parts in shards:
        heights = jax.random.uniform(jax.random.fold_in(jax.random.fold_in(stream_key, 6), dim), (parts,), jnp.float32, smallest / len(shards), largest / len(shards))
        factor_of = factor_of * jnp.repeat(jnp.exp(heights), shape[dim] // parts).reshape((-1,) + (1,) * (len(shape) - 1 - dim))
    return factor_of


def bell_draw(stream_key, extent, spread, bound, shards=(), dtype=jnp.bfloat16):
    factor_of = shard_levels(stream_key, extent, shards, -0.22, 0.18) if shards else 1.0
    values = jax.random.normal(stream_key, extent, jnp.float32) * spread * factor_of
    return jnp.minimum(jnp.maximum(values, -bound), bound).astype(dtype)


def setup_inputs(seed: int = 0, part: int = 0) -> dict:
    key_list = jax.random.split(jax.random.key(seed), 7)
    part_keys = jax.random.split(jax.random.fold_in(key_list[6], part), 7)
    return {
        "innovations": bell_draw(part_keys[0], (FRONTS, SECTIONS, C, LATS, WIN), 1.0, 6.0, ((1, 2), (3, 8))),
        "obs_mask": set_ends((jax.random.randint(part_keys[1], (SECTIONS, LATS // 4, WIN // 32), 0, 2) < 1).astype(jnp.int32), jax.random.fold_in(part_keys[1], 1), 0, 1),
        "slopes": jnp.clip(-0.14941406 + 1.2431641 * jax.random.uniform(part_keys[2], (SECTIONS, HID, LATS, WIN), jnp.float32) ** shard_levels(part_keys[2], (SECTIONS, HID, LATS, WIN), ((0, 2), (1, 2), (2, 4)), -0.2, 0.2), -0.14941406, 1.09375).astype(jnp.bfloat16),
        "layer_of": jax.random.randint(key_list[3], (SECTIONS,), 0, LAYERS).astype(jnp.int32),
        "weight_in": bell_draw(key_list[4], (LAYERS, 3, 3, C, HID), (9 * HID) ** -0.5, 0.1875, ((4, 2),)),
        "weight_out": bell_draw(key_list[5], (LAYERS, 3, 3, HID, C), (9 * C) ** -0.5, 0.25, ((3, 2),)),
    }


def spread_tiles(obs_tiles):
    return jnp.repeat(jnp.repeat(obs_tiles, 4, axis=-2), 32, axis=-1).astype(jnp.float32)


def transposed_conv(field, kernel):
    height = field.shape[2]
    width = field.shape[3]
    padded = jnp.pad(field.astype(jnp.float32), ((0, 0), (0, 0), (1, 1), (1, 1)))
    summed = None
    for row_off in range(3):
        for col_off in range(3):
            shifted = padded[:, :, 2 - row_off:2 - row_off + height, 2 - col_off:2 - col_off + width]
            contrib = jnp.einsum('ij,fjhw->fihw', kernel[row_off, col_off].astype(jnp.float32), shifted, precision=lax.Precision.HIGHEST)
            summed = contrib if summed is None else summed + contrib
    return summed


def reference(innovations, obs_mask, slopes, layer_of, weight_in, weight_out):
    forcing = innovations.astype(jnp.float32) * spread_tiles(obs_mask)[None, :, None]
    adjoint = jnp.zeros((FRONTS, C, LATS, WIN), jnp.float32)
    fresh = [None] * SECTIONS
    for section in reversed(range(SECTIONS)):
        layer_no = layer_of[section]
        rounded = adjoint.astype(jnp.bfloat16)
        hidden_grad = transposed_conv(rounded, weight_out[layer_no])
        scaled = (slopes[section].astype(jnp.float32)[None] * hidden_grad).astype(jnp.bfloat16)
        adjoint = adjoint + transposed_conv(scaled, weight_in[layer_no]) + forcing[:, section]
        fresh[section] = adjoint
    return jnp.stack(fresh, axis=1)
```

```python
import functools

import jax
import jax.numpy as jnp
from jax import lax
from jax.experimental import pallas as pl
from jax.experimental.pallas import tpu as pltpu
from jax.sharding import PartitionSpec as P


def swap_chan(block):
    return lax.ppermute(block, "chan", [(0, 1), (1, 0)])


def swap_lat(block):
    bands = lax.axis_size("lat")
    pairs = []
    for band in range(bands - 1):
        pairs += [(2 * band + 1, 2 * band + 2), (2 * band + 2, 2 * band + 1)]
    return lax.ppermute(block, ("lat", "chan"), pairs)


def to_earlier(block):
    count = lax.axis_size("tm")
    return lax.ppermute(block, "tm", [(i, i - 1) for i in range(1, count)])


def lane_shift(values, step):
    lanes = lax.broadcasted_iota(jnp.int32, values.shape, 1)
    edge = 0 if step == 1 else values.shape[1] - 1
    rolled = pltpu.roll(values, step % values.shape[1], 1)
    return jnp.where(lanes == edge, 0.0, rolled)


def step_kernel(
    dims, chan_ref, mask_ref, halo_ref, outer_ref, inner_ref, other_ref, innov_ref,
    slope_own_ref, slope_other_ref, slope_halo_ref,
    out_own_ref, out_other_ref, in_own_ref, in_other_ref,
    result_ref, field, hidden_own, hidden_other,
):
    fronts, states, pitch, half, cells = dims
    chan = chan_ref[0]
    rows = 4
    field[...] = jnp.zeros_like(field)
    for spot, piece in enumerate((halo_ref, outer_ref, inner_ref, other_ref)):
        place = spot + chan * (3 - 2 * spot)
        for i in range(2):
            start = pl.multiple_of(place * (2 * pitch) + i * pitch, 16)
            field[pl.ds(start, states), :] = piece[i]

    for j in range(rows + 2):
        near = field[j * pitch:(j + 3) * pitch, :]
        lat_row = jnp.clip(4 * chan + j - 1, 0, 7)
        for kernel_ref, slope_ref, hidden, part in (
            (out_own_ref, slope_own_ref, hidden_own, 0),
            (out_other_ref, slope_other_ref, hidden_other, 1),
        ):
            taps = jnp.dot(kernel_ref[...], near, preferred_element_type=jnp.float32)
            slope = slope_ref[lat_row].astype(jnp.float32)
            if j in (0, rows + 1):
                outside = chan == (0 if j == 0 else 1)
                edge = slope_halo_ref[(1 - part) * half:(2 - part) * half, :].astype(jnp.float32)
                slope = jnp.where(outside, edge, slope)
            for f in range(fronts):
                lanes = slice(f * cells, (f + 1) * cells)
                total = (
                    taps[half:2 * half, lanes]
                    + lane_shift(taps[0:half, lanes], -1)
                    + lane_shift(taps[2 * half:3 * half, lanes], 1)
                )
                hidden[j * half:(j + 1) * half, lanes] = (slope * total).astype(jnp.bfloat16)

    for h in range(rows):
        taps = jnp.dot(
            in_own_ref[...], hidden_own[h * half:(h + 3) * half, :], preferred_element_type=jnp.float32
        ) + jnp.dot(
            in_other_ref[...], hidden_other[h * half:(h + 3) * half, :], preferred_element_type=jnp.float32
        )
        before = field[(h + 2) * pitch:(h + 3) * pitch, :].astype(jnp.float32)
        for f in range(fronts):
            lanes = slice(f * cells, (f + 1) * cells)
            total = (
                before[:, lanes]
                + taps[pitch:2 * pitch, lanes]
                + lane_shift(taps[0:pitch, lanes], -1)
                + lane_shift(taps[2 * pitch:3 * pitch, lanes], 1)
            )
            result_ref[pl.ds(f * states * rows + h, states, stride=rows), :] = total[:states]

    tile = lax.broadcasted_iota(jnp.int32, (1, cells), 1) // 32
    seen = jnp.zeros((1, cells), jnp.float32)
    for t in range(cells // 32):
        seen = jnp.where(tile == t, mask_ref[t].astype(jnp.float32), seen)
    result_ref[...] += innov_ref[...].astype(jnp.float32) * seen


def per_device(innovations, obs_mask, slopes, layer_of, weight_in, weight_out):
    fronts, _, states, rows, cells = innovations.shape
    half = slopes.shape[1]
    pitch = -(-states // 16) * 16
    owners = lax.axis_size("tm")
    chan = lax.axis_index("chan")

    seen = jnp.repeat(obs_mask[0, 0], 32).astype(jnp.bfloat16)

    def to_send(adjoint):
        field = adjoint.transpose(2, 1, 0, 3).reshape(rows, states, fronts * cells)
        return (
            lax.dynamic_slice_in_dim(field, 2 * chan, 2),
            lax.dynamic_slice_in_dim(field, 2 - 2 * chan, 2),
        )

    outer, inner = to_send(innovations[:, 0] * seen)
    layer = layer_of[lax.axis_index("tm")]
    k_out = lax.dynamic_index_in_dim(weight_out, layer, 0, keepdims=False)
    k_in = lax.dynamic_index_in_dim(weight_in, layer, 0, keepdims=False)
    lap = ((0, 0),) * 3 + ((0, pitch - states),)
    out_own = jnp.pad(k_out[::-1].transpose(1, 2, 0, 3), lap).reshape(3 * half, 3 * pitch)
    in_own = jnp.pad(k_in[::-1].transpose(0, 3, 1, 2), lap).reshape(3 * half, 3 * pitch).T
    slope_own = slopes[0].transpose(1, 0, 2)
    out_other = swap_chan(out_own)
    in_other = swap_chan(in_own)
    slope_other = swap_chan(slope_own)
    edge = jnp.concatenate([slope_own, slope_other], axis=1)
    edge = lax.dynamic_index_in_dim(edge, 7 * chan, 0, keepdims=False)
    slope_halo = swap_lat(edge)

    vm = pl.BlockSpec(memory_space=pltpu.VMEM)
    sm = pl.BlockSpec(memory_space=pltpu.SMEM)
    step = pl.pallas_call(
        functools.partial(step_kernel, (fronts, states, pitch, half, cells)),
        out_shape=jax.ShapeDtypeStruct((fronts * states * rows, cells), jnp.float32),
        in_specs=[sm, sm] + [vm] * 12,
        out_specs=vm,
        scratch_shapes=[
            pltpu.VMEM((8 * pitch, fronts * cells), jnp.bfloat16),
            pltpu.VMEM((6 * half, fronts * cells), jnp.bfloat16),
            pltpu.VMEM((6 * half, fronts * cells), jnp.bfloat16),
        ],
        compiler_params=pltpu.CompilerParams(vmem_limit_bytes=32 << 20),
    )
    for hop in range(1, owners):
        outer_in = to_earlier(outer)
        inner_in = to_earlier(inner)
        halo = swap_lat(outer_in)
        other = swap_chan(inner_in)
        result = step(
            chan.reshape(1), obs_mask[0, 0], halo, outer_in, inner_in, other,
            innovations.reshape(fronts * states * rows, cells),
            slope_own, slope_other, slope_halo, out_own, out_other, in_own, in_other,
        )
        if hop + 1 < owners:
            outer, inner = to_send(result.reshape(innovations.shape)[:, 0].astype(jnp.bfloat16))
    return result.reshape(innovations.shape)


def solution(mesh):
    return jax.shard_map(
        per_device,
        mesh=mesh,
        in_specs=(
            P(None, ("grp", "tm"), None, ("lat", "chan"), None),
            P(("grp", "tm"), ("lat", "chan"), None),
            P(("grp", "tm"), "chan", "lat", None),
            P(),
            P(None, None, None, None, "chan"),
            P(None, None, None, "chan", None),
        ),
        out_specs=P(None, ("grp", "tm"), None, ("lat", "chan"), None),
        check_vma=False,
    )
```

```python
import functools

import jax
import jax.numpy as jnp
from jax import lax
from jax.experimental import pallas as pl
from jax.experimental.pallas import tpu as pltpu
from jax.sharding import PartitionSpec as P

VMEM = pl.BlockSpec(memory_space=pltpu.VMEM)
HBM = pl.BlockSpec(memory_space=pltpu.HBM)


def swap_chan(block):
    return lax.ppermute(block, "chan", [(0, 1), (1, 0)])


def swap_lat(block):
    bands, groups = lax.axis_size("lat"), lax.axis_size("grp")
    last = 2 * bands - 1
    pairs = []
    for group in range(groups):
        for i in range(1, last, 2):
            pairs += [(group, i, group, i + 1), (group, i + 1, group, i)]
        mate = group ^ 1 if group ^ 1 < groups else group
        pairs += [(group, 0, mate, 0), (group, last, mate, last)]
    route = [(g * 2 * bands + i, m * 2 * bands + k) for g, i, m, k in pairs]
    return lax.ppermute(block, ("grp", "lat", "chan"), route)


def to_earlier(block):
    count = lax.axis_size("tm")
    return lax.ppermute(block, "tm", [(i, (i - 1) % count) for i in range(count)])


def lane_shift(values, step):
    lanes = lax.broadcasted_iota(jnp.int32, values.shape, 1)
    edge = 0 if step == 1 else values.shape[1] - 1
    return jnp.where(lanes == edge, 0.0, pltpu.roll(values, step % values.shape[1], 1))


def tile_mask(mask_ref, cells):
    tile = lax.broadcasted_iota(jnp.int32, (1, cells), 1) // 32
    seen = jnp.zeros((1, cells), jnp.float32)
    for t in range(cells // 32):
        seen = jnp.where(tile == t, mask_ref[t].astype(jnp.float32), seen)
    return seen


def split_rows(dims, wide, outer_ref, inner_ref):
    fronts, states, cells = dims
    chan = lax.axis_index("chan")
    for piece, first in ((outer_ref, 2 * chan), (inner_ref, 2 - 2 * chan)):
        for i in range(2):
            for f in range(fronts):
                rows = wide[pl.ds(f * states * 4 + first + i, states, stride=4), :]
                piece[i, :, f * cells:(f + 1) * cells] = rows.astype(jnp.bfloat16)


def split_kernel(dims, state_ref, outer_ref, inner_ref, wide):
    wide[...] = state_ref[...]
    split_rows(dims, wide, outer_ref, inner_ref)


def first_kernel(
    dims, layer_ref, mask_ref, innov_ref, slope_ref, out_ref, in_ref,
    outer_ref, inner_ref, forcing_ref, raw_ref,
    layers, mask, innov, slope, taps_out, taps_in, wide, sem,
):
    fronts, states, cells, half = dims

    def fetch(i, src, dst):
        copy = pltpu.make_async_copy(src, dst, sem.at[i])
        copy.start()
        return copy

    fetches = [
        fetch(i, src, dst)
        for i, (src, dst) in enumerate(
            ((layer_ref, layers), (mask_ref, mask), (innov_ref, innov), (slope_ref, slope))
        )
    ]
    fetches[0].wait()
    layer = layers[lax.axis_index("tm")]
    fetches += [fetch(4, out_ref.at[layer], taps_out), fetch(5, in_ref.at[layer], taps_in)]
    fetches[1].wait()
    fetches[2].wait()
    wide[...] = innov[...].astype(jnp.float32) * tile_mask(mask, cells)
    split_rows((fronts, states, cells), wide, outer_ref, inner_ref)
    forcing_ref[...] = wide[...].astype(jnp.bfloat16)
    fetches[3].wait()
    raw_ref[18 * half:, :] = slope[...]
    for i, taps in enumerate((taps_out, taps_in)):
        fetches[4 + i].wait()
        for t in range(9):
            start = (9 * i + t) * half
            raw_ref[start:start + half, :states] = taps[t // 3, t % 3]


def order_kernel(dims, own_ref, away_ref, first_ref, second_ref, slope_ref, edge_ref, wide):
    states, pitch, half, cells = dims
    hidden, lanes = 2 * half, 2 * cells
    chan = lax.axis_index("chan")
    inside = lax.broadcasted_iota(jnp.int32, (half, lanes), 1) < states

    def placed(raw_ref, i, a, b, spot):
        start = (9 * i + 3 * a + b) * half
        block = raw_ref[start:start + half, :].astype(jnp.float32)
        block = jnp.where(inside, jnp.concatenate([block, block], axis=1), 0.0)
        return block if spot == 0 else pltpu.roll(block, spot * pitch, 1)

    turned = [[None, None] for _ in range(3)]
    for part, raw_ref in enumerate((own_ref, away_ref)):
        for b in range(3):
            rows = sum(placed(raw_ref, 0, a, b, 2 - a) for a in range(3))
            start = b * hidden + part * half
            first_ref[start:start + half, :] = rows.astype(jnp.bfloat16)
        for a in range(3):
            turned[2 - a][part] = sum(placed(raw_ref, 1, a, b, b) for b in range(3))
        wide[...] = raw_ref[18 * half:, :].astype(jnp.float32)
        for j in range(6):
            lat_row = jnp.clip(4 * chan + j - 1, 0, 7)
            start = j * hidden + part * half
            slope_ref[start:start + half, :] = wide[pl.ds(lat_row, half, stride=8), :].astype(jnp.bfloat16)
        start = (1 - part) * half
        edge_ref[start:start + half, :] = wide[pl.ds(7 * chan, half, stride=8), :].astype(jnp.bfloat16)
    turned = jnp.concatenate([block for pair in turned for block in pair], axis=0).T
    second_ref[...] = turned[:3 * pitch].astype(jnp.bfloat16)


def step_kernel(
    dims, halo_ref, outer_ref, inner_ref, other_ref, forcing_ref,
    first_ref, second_ref, slope_ref, edge_ref, result_ref, field, hidden_grad,
):
    fronts, states, pitch, hidden, cells = dims
    chan, band = lax.axis_index("chan"), lax.axis_index("lat")
    rows = 4
    live = lax.axis_index("tm") < lax.axis_size("tm") - 1
    border = (band == 0) & (chan == 0) | (band == lax.axis_size("lat") - 1) & (chan == 1)
    field[...] = jnp.zeros_like(field)
    for spot, piece in enumerate((halo_ref, outer_ref, inner_ref, other_ref)):

        @pl.when(live & ~border if spot == 0 else live)
        def _():
            place = spot + chan * (3 - 2 * spot)
            for i in range(2):
                start = pl.multiple_of(place * (2 * pitch) + i * pitch, 16)
                field[pl.ds(start, states), :] = piece[i]

    for j in range(rows + 2):
        taps = jnp.dot(
            first_ref[:, :3 * pitch], field[j * pitch:(j + 3) * pitch, :],
            preferred_element_type=jnp.float32,
        )
        slope = slope_ref[j * hidden:(j + 1) * hidden, :].astype(jnp.float32)
        if j in (0, rows + 1):
            beyond = jnp.where(border, 0.0, edge_ref[...].astype(jnp.float32))
            slope = jnp.where(chan == (0 if j == 0 else 1), beyond, slope)
        for f in range(fronts):
            lanes = slice(f * cells, (f + 1) * cells)
            total = (
                taps[hidden:2 * hidden, lanes]
                + lane_shift(taps[0:hidden, lanes], -1)
                + lane_shift(taps[2 * hidden:3 * hidden, lanes], 1)
            )
            hidden_grad[j * hidden:(j + 1) * hidden, lanes] = (slope * total).astype(jnp.bfloat16)

    result_ref[...] = forcing_ref[...].astype(jnp.float32)
    for h in range(rows):
        taps = jnp.dot(
            second_ref[...], hidden_grad[h * hidden:(h + 3) * hidden, :],
            preferred_element_type=jnp.float32,
        )
        before = field[(h + 2) * pitch:(h + 3) * pitch, :].astype(jnp.float32)
        for f in range(fronts):
            lanes = slice(f * cells, (f + 1) * cells)
            total = (
                before[:, lanes]
                + taps[pitch:2 * pitch, lanes]
                + lane_shift(taps[0:pitch, lanes], -1)
                + lane_shift(taps[2 * pitch:3 * pitch, lanes], 1)
            )
            spots = pl.ds(f * states * rows + h, states, stride=rows)
            result_ref[spots, :] = result_ref[spots, :] + total[:states]


def per_device(innovations, obs_mask, slopes, layer_of, weight_in, weight_out):
    fronts, _, states, rows, cells = innovations.shape
    half = slopes.shape[1]
    hidden = 2 * half
    pitch = -(-states // 16) * 16
    owners = lax.axis_size("tm")
    flat = (fronts * states * rows, cells)

    def array(shape, dtype=jnp.bfloat16):
        return jax.ShapeDtypeStruct(shape, dtype)

    piece = array((2, states, fronts * cells))
    modest = pltpu.CompilerParams(vmem_limit_bytes=8 << 20)
    outer, inner, forcing, raw_own = pl.pallas_call(
        functools.partial(first_kernel, (fronts, states, cells, half)),
        out_shape=(piece, piece, array(flat), array((26 * half, cells))),
        in_specs=[HBM] * 6,
        out_specs=(VMEM,) * 4,
        scratch_shapes=[
            pltpu.SMEM(layer_of.shape, jnp.int32),
            pltpu.SMEM(obs_mask.shape[2:], jnp.int32),
            pltpu.VMEM(flat, jnp.bfloat16),
            pltpu.VMEM((8 * half, cells), jnp.bfloat16),
            pltpu.VMEM((3, 3, half, states), jnp.bfloat16),
            pltpu.VMEM((3, 3, half, states), jnp.bfloat16),
            pltpu.VMEM(flat, jnp.float32),
            pltpu.SemaphoreType.DMA((6,)),
        ],
        compiler_params=modest,
    )(
        *(
            pltpu.with_memory_space_constraint(argument, pltpu.HBM)
            for argument in (
                layer_of, obs_mask[0, 0], innovations.reshape(flat), slopes.reshape(8 * half, cells),
                weight_out, weight_in.transpose(0, 1, 2, 4, 3),
            )
        )
    )
    outer_in = to_earlier(outer)
    raw_away = swap_chan(raw_own)
    first, second, slope, edge = pl.pallas_call(
        functools.partial(order_kernel, (states, pitch, half, cells)),
        out_shape=(
            array((3 * hidden, 2 * cells)), array((3 * pitch, 3 * hidden)),
            array((6 * hidden, cells)), array((hidden, cells)),
        ),
        in_specs=[VMEM] * 2,
        out_specs=(VMEM,) * 4,
        scratch_shapes=[pltpu.VMEM((8 * half, cells), jnp.float32)],
        compiler_params=modest,
    )(raw_own, raw_away)
    edge, inner = lax.optimization_barrier((edge, inner))
    inner_in = to_earlier(inner)
    edge = swap_lat(edge)
    edge, outer_in = lax.optimization_barrier((edge, outer_in))

    for hop in range(1, owners):
        if hop > 1:
            outer, inner = pl.pallas_call(
                functools.partial(split_kernel, (fronts, states, cells)),
                out_shape=(piece, piece),
                in_specs=[VMEM],
                out_specs=(VMEM, VMEM),
                scratch_shapes=[pltpu.VMEM(flat, jnp.float32)],
                compiler_params=modest,
            )(result)
            outer_in, inner_in = to_earlier(outer), to_earlier(inner)
        halo = swap_lat(outer_in)
        other = swap_chan(inner_in)
        result = pl.pallas_call(
            functools.partial(step_kernel, (fronts, states, pitch, hidden, cells)),
            out_shape=array(flat, jnp.float32),
            in_specs=[VMEM] * 9,
            out_specs=VMEM,
            scratch_shapes=[
                pltpu.VMEM((8 * pitch, fronts * cells), jnp.bfloat16),
                pltpu.VMEM((6 * hidden, fronts * cells), jnp.bfloat16),
            ],
            compiler_params=modest,
        )(halo, outer_in, inner_in, other, forcing, first, second, slope, edge)
    return result.reshape(innovations.shape)


def solution(mesh):
    return jax.shard_map(
        per_device,
        mesh=mesh,
        in_specs=(
            P(None, ("grp", "tm"), None, ("lat", "chan"), None),
            P(("grp", "tm"), ("lat", "chan"), None),
            P(("grp", "tm"), "chan", "lat", None),
            P(),
            P(None, None, None, None, "chan"),
            P(None, None, None, "chan", None),
        ),
        out_specs=P(None, ("grp", "tm"), None, ("lat", "chan"), None),
        check_vma=False,
    )
```

```python
import functools

import jax
import jax.numpy as jnp
from jax import lax
from jax.experimental import pallas as pl
from jax.experimental.pallas import tpu as pltpu
from jax.sharding import PartitionSpec as P

VMEM = pl.BlockSpec(memory_space=pltpu.VMEM)
HBM = pl.BlockSpec(memory_space=pltpu.HBM)


def swap_chan(block):
    return lax.ppermute(block, "chan", [(0, 1), (1, 0)])


def swap_lat(block):
    bands, groups = lax.axis_size("lat"), lax.axis_size("grp")
    last = 2 * bands - 1
    pairs = []
    for group in range(groups):
        for i in range(1, last, 2):
            pairs += [(group, i, group, i + 1), (group, i + 1, group, i)]
        mate = group ^ 1 if group ^ 1 < groups else group
        pairs += [(group, 0, mate, 0), (group, last, mate, last)]
    route = [(g * 2 * bands + i, m * 2 * bands + k) for g, i, m, k in pairs]
    return lax.ppermute(block, ("grp", "lat", "chan"), route)


def to_earlier(block):
    count = lax.axis_size("tm")
    return lax.ppermute(block, "tm", [(i, (i - 1) % count) for i in range(count)])


def lane_shift(values, step):
    lanes = lax.broadcasted_iota(jnp.int32, values.shape, 1)
    edge = 0 if step == 1 else values.shape[1] - 1
    return jnp.where(lanes == edge, 0.0, pltpu.roll(values, step % values.shape[1], 1))


def tile_mask(mask_ref, cells):
    tile = lax.broadcasted_iota(jnp.int32, (1, cells), 1) // 32
    seen = jnp.zeros((1, cells), jnp.float32)
    for t in range(cells // 32):
        seen = jnp.where(tile == t, mask_ref[t].astype(jnp.float32), seen)
    return seen


def split_rows(dims, wide, piece, outer_ref, inner_ref):
    fronts, states, cells = dims
    chan = lax.axis_index("chan")
    for ref, first in ((outer_ref, 2 * chan), (inner_ref, 2 - 2 * chan)):
        for i in range(2):
            for f in range(fronts):
                rows = wide[pl.ds(f * states * 4 + first + i, states, stride=4), :]
                piece[pl.ds(i * fronts + f, states, stride=2 * fronts), :] = rows
        ref[...] = piece[...].astype(jnp.bfloat16)


def spread_rows(dims, ref, piece, field, start, used):
    fronts, states, pitch, cells = dims
    piece[...] = jnp.where(used, ref[...].astype(jnp.float32), 0.0)
    for i in range(2):
        for f in range(fronts):
            rows = piece[pl.ds(i * fronts + f, states, stride=2 * fronts), :]
            spot = pl.ds(pl.multiple_of(start + i * pitch, 16), states)
            field[spot, f * cells:(f + 1) * cells] = rows.astype(jnp.bfloat16)


def split_kernel(dims, state_ref, outer_ref, inner_ref, wide, piece):
    wide[...] = state_ref[...]
    split_rows(dims, wide, piece, outer_ref, inner_ref)


def first_kernel(
    dims, layer_ref, mask_ref, innov_ref, slope_ref, out_ref, in_ref,
    outer_ref, inner_ref, forcing_ref, raw_ref,
    layers, mask, innov, slope, taps_out, taps_in, wide, piece, sem,
):
    fronts, states, cells, half = dims

    def fetch(i, src, dst):
        copy = pltpu.make_async_copy(src, dst, sem.at[i])
        copy.start()
        return copy

    fetches = [
        fetch(i, src, dst)
        for i, (src, dst) in enumerate(
            ((layer_ref, layers), (mask_ref, mask), (innov_ref, innov), (slope_ref, slope))
        )
    ]
    fetches[0].wait()
    layer = layers[lax.axis_index("tm")]
    fetches += [fetch(4, out_ref.at[layer], taps_out), fetch(5, in_ref.at[layer], taps_in)]
    fetches[1].wait()
    fetches[2].wait()
    wide[...] = innov[...].astype(jnp.float32) * tile_mask(mask, cells)
    split_rows((fronts, states, cells), wide, piece, outer_ref, inner_ref)
    forcing_ref[...] = wide[...].astype(jnp.bfloat16)
    fetches[3].wait()
    raw_ref[18 * half:, :] = slope[...]
    for i, taps in enumerate((taps_out, taps_in)):
        fetches[4 + i].wait()
        for t in range(9):
            start = (9 * i + t) * half
            raw_ref[start:start + half, :states] = taps[t // 3, t % 3]


def order_kernel(dims, own_ref, away_ref, first_ref, second_ref, slope_ref, edge_ref, wide):
    states, pitch, half, cells = dims
    hidden, lanes = 2 * half, 2 * cells
    chan = lax.axis_index("chan")
    inside = lax.broadcasted_iota(jnp.int32, (half, lanes), 1) < states

    def placed(raw_ref, i, a, b, spot):
        start = (9 * i + 3 * a + b) * half
        block = raw_ref[start:start + half, :].astype(jnp.float32)
        block = jnp.where(inside, jnp.concatenate([block, block], axis=1), 0.0)
        return block if spot == 0 else pltpu.roll(block, spot * pitch, 1)

    turned = [[None, None] for _ in range(3)]
    for part, raw_ref in enumerate((own_ref, away_ref)):
        for b in range(3):
            rows = sum(placed(raw_ref, 0, a, b, 2 - a) for a in range(3))
            start = b * hidden + part * half
            first_ref[start:start + half, :] = rows.astype(jnp.bfloat16)
        for a in range(3):
            turned[2 - a][part] = sum(placed(raw_ref, 1, a, b, b) for b in range(3))
        wide[...] = raw_ref[18 * half:, :].astype(jnp.float32)
        for j in range(6):
            lat_row = jnp.clip(4 * chan + j - 1, 0, 7)
            start = j * hidden + part * half
            slope_ref[start:start + half, :] = wide[pl.ds(lat_row, half, stride=8), :].astype(jnp.bfloat16)
        start = (1 - part) * half
        edge_ref[start:start + half, :] = wide[pl.ds(7 * chan, half, stride=8), :].astype(jnp.bfloat16)
    turned = jnp.concatenate([block for pair in turned for block in pair], axis=0).T
    second_ref[...] = turned[:3 * pitch].astype(jnp.bfloat16)


def hidden_row(dims, j, first_ref, slope, field, hidden_grad, spot):
    fronts, pitch, hidden, cells = dims
    for pair in range(fronts // 2):
        taps = jnp.dot(
            first_ref[:, :3 * pitch],
            field[j * pitch:(j + 3) * pitch, 2 * pair * cells:2 * (pair + 1) * cells],
            preferred_element_type=jnp.float32,
        )
        for f in range(2):
            lanes = slice(f * cells, (f + 1) * cells)
            total = (
                taps[hidden:2 * hidden, lanes]
                + lane_shift(taps[0:hidden, lanes], -1)
                + lane_shift(taps[2 * hidden:3 * hidden, lanes], 1)
            )
            start = (2 * pair + f) * cells
            hidden_grad[spot:spot + hidden, start:start + cells] = (slope * total).astype(jnp.bfloat16)


def own_kernel(
    dims, outer_ref, inner_ref, first_ref, slope_ref, field_ref, hidden_ref, piece,
):
    fronts, states, pitch, hidden, cells = dims
    chan = lax.axis_index("chan")
    live = lax.axis_index("tm") < lax.axis_size("tm") - 1
    field_ref[...] = jnp.zeros_like(field_ref)
    for ref, start in ((outer_ref, chan * 2 * pitch), (inner_ref, (1 - chan) * 2 * pitch)):
        spread_rows((fronts, states, pitch, cells), ref, piece, field_ref, start, live)
    for j in range(2):
        slope = slope_ref[(j + 2) * hidden:(j + 3) * hidden, :].astype(jnp.float32)
        hidden_row((fronts, pitch, hidden, cells), j, first_ref, slope, field_ref, hidden_ref, j * hidden)


def step_kernel(
    dims, halo_ref, other_ref, own_ref, middle_ref, forcing_ref,
    first_ref, second_ref, slope_ref, edge_ref, result_ref, field, hidden_grad, piece, result, sem,
):
    fronts, states, pitch, hidden, cells = dims
    chan, band = lax.axis_index("chan"), lax.axis_index("lat")
    rows = 4
    live = lax.axis_index("tm") < lax.axis_size("tm") - 1
    border = (band == 0) & (chan == 0) | (band == lax.axis_size("lat") - 1) & (chan == 1)
    field[...] = jnp.zeros_like(field)
    for ref, start, used in (
        (halo_ref, chan * 6 * pitch, live & ~border),
        (other_ref, (1 - chan) * 6 * pitch, live),
    ):
        spread_rows((fronts, states, pitch, cells), ref, piece, field, start, used)
    field[2 * pitch:6 * pitch, :] = own_ref[...]
    hidden_grad[2 * hidden:4 * hidden, :] = middle_ref[...]
    for j in (0, 1, rows, rows + 1):
        slope = slope_ref[j * hidden:(j + 1) * hidden, :].astype(jnp.float32)
        if j in (0, rows + 1):
            beyond = jnp.where(border, 0.0, edge_ref[...].astype(jnp.float32))
            slope = jnp.where(chan == (0 if j == 0 else 1), beyond, slope)
        hidden_row((fronts, pitch, hidden, cells), j, first_ref, slope, field, hidden_grad, j * hidden)

    size = 2 * states * rows
    copies = []
    for pair in range(fronts // 2):
        part = slice(pair * size, (pair + 1) * size)
        result[part, :] = forcing_ref[part, :].astype(jnp.float32)
        block = slice(2 * pair * cells, 2 * (pair + 1) * cells)
        for h in range(rows):
            taps = jnp.dot(
                second_ref[...], hidden_grad[h * hidden:(h + 3) * hidden, block],
                preferred_element_type=jnp.float32,
            )
            before = field[(h + 2) * pitch:(h + 3) * pitch, block].astype(jnp.float32)
            for f in range(2):
                lanes = slice(f * cells, (f + 1) * cells)
                total = (
                    before[:, lanes]
                    + taps[pitch:2 * pitch, lanes]
                    + lane_shift(taps[0:pitch, lanes], -1)
                    + lane_shift(taps[2 * pitch:3 * pitch, lanes], 1)
                )
                spots = pl.ds((2 * pair + f) * states * rows + h, states, stride=rows)
                result[spots, :] = result[spots, :] + total[:states]
        copies.append(pltpu.make_async_copy(result.at[part], result_ref.at[part], sem.at[pair]))
        copies[-1].start()
    for copy in copies:
        copy.wait()


def per_device(innovations, obs_mask, slopes, layer_of, weight_in, weight_out):
    fronts, _, states, rows, cells = innovations.shape
    half = slopes.shape[1]
    hidden = 2 * half
    pitch = -(-states // 16) * 16
    owners = lax.axis_size("tm")
    flat = (fronts * states * rows, cells)

    def array(shape, dtype=jnp.bfloat16):
        return jax.ShapeDtypeStruct(shape, dtype)

    piece = array((2 * states * fronts, cells))
    piece_wide = pltpu.VMEM(piece.shape, jnp.float32)
    field_shape, hidden_shape = (8 * pitch, fronts * cells), (6 * hidden, fronts * cells)
    modest = pltpu.CompilerParams(vmem_limit_bytes=8 << 20)
    outer, inner, forcing, raw_own = pl.pallas_call(
        functools.partial(first_kernel, (fronts, states, cells, half)),
        out_shape=(piece, piece, array(flat), array((26 * half, cells))),
        in_specs=[HBM] * 6,
        out_specs=(VMEM,) * 4,
        scratch_shapes=[
            pltpu.SMEM(layer_of.shape, jnp.int32),
            pltpu.SMEM(obs_mask.shape[2:], jnp.int32),
            pltpu.VMEM(flat, jnp.bfloat16),
            pltpu.VMEM((8 * half, cells), jnp.bfloat16),
            pltpu.VMEM((3, 3, half, states), jnp.bfloat16),
            pltpu.VMEM((3, 3, half, states), jnp.bfloat16),
            pltpu.VMEM(flat, jnp.float32),
            piece_wide,
            pltpu.SemaphoreType.DMA((6,)),
        ],
        compiler_params=modest,
    )(
        *(
            pltpu.with_memory_space_constraint(argument, pltpu.HBM)
            for argument in (
                layer_of, obs_mask[0, 0], innovations.reshape(flat), slopes.reshape(8 * half, cells),
                weight_out, weight_in.transpose(0, 1, 2, 4, 3),
            )
        )
    )
    outer_in = to_earlier(outer)
    raw_away = swap_chan(raw_own)
    first, second, slope, edge = pl.pallas_call(
        functools.partial(order_kernel, (states, pitch, half, cells)),
        out_shape=(
            array((3 * hidden, 2 * cells)), array((3 * pitch, 3 * hidden)),
            array((6 * hidden, cells)), array((hidden, cells)),
        ),
        in_specs=[VMEM] * 2,
        out_specs=(VMEM,) * 4,
        scratch_shapes=[pltpu.VMEM((8 * half, cells), jnp.float32)],
        compiler_params=modest,
    )(raw_own, raw_away)
    edge, inner = lax.optimization_barrier((edge, inner))
    inner_in = to_earlier(inner)
    edge = swap_lat(edge)
    edge, outer_in = lax.optimization_barrier((edge, outer_in))

    for hop in range(1, owners):
        if hop > 1:
            outer, inner = pl.pallas_call(
                functools.partial(split_kernel, (fronts, states, cells)),
                out_shape=(piece, piece),
                in_specs=[VMEM],
                out_specs=(VMEM, VMEM),
                scratch_shapes=[pltpu.VMEM(flat, jnp.float32), piece_wide],
                compiler_params=modest,
            )(result)
            outer_in, inner_in = to_earlier(outer), to_earlier(inner)
        halo = swap_lat(outer_in)
        other = swap_chan(inner_in)
        sizes = (fronts, states, pitch, hidden, cells)
        own, middle = pl.pallas_call(
            functools.partial(own_kernel, sizes),
            out_shape=(array((4 * pitch, fronts * cells)), array((2 * hidden, fronts * cells))),
            in_specs=[VMEM] * 4,
            out_specs=(VMEM, VMEM),
            scratch_shapes=[piece_wide],
            compiler_params=modest,
        )(outer_in, inner_in, first, slope)
        result = pl.pallas_call(
            functools.partial(step_kernel, sizes),
            out_shape=array(flat, jnp.float32),
            in_specs=[VMEM] * 9,
            out_specs=HBM,
            scratch_shapes=[
                pltpu.VMEM(field_shape, jnp.bfloat16),
                pltpu.VMEM(hidden_shape, jnp.bfloat16),
                piece_wide,
                pltpu.VMEM(flat, jnp.float32),
                pltpu.SemaphoreType.DMA((fronts // 2,)),
            ],
            compiler_params=modest,
        )(halo, other, own, middle, forcing, first, second, slope, edge)
    return result.reshape(innovations.shape)


def solution(mesh):
    return jax.shard_map(
        per_device,
        mesh=mesh,
        in_specs=(
            P(None, ("grp", "tm"), None, ("lat", "chan"), None),
            P(("grp", "tm"), ("lat", "chan"), None),
            P(("grp", "tm"), "chan", "lat", None),
            P(),
            P(None, None, None, None, "chan"),
            P(None, None, None, "chan", None),
        ),
        out_specs=P(None, ("grp", "tm"), None, ("lat", "chan"), None),
        check_vma=False,
    )
```

```python
import functools

import jax
import jax.numpy as jnp
from jax import lax
from jax.experimental import pallas as pl
from jax.experimental.pallas import tpu as pltpu
from jax.sharding import PartitionSpec as P

VMEM = pl.BlockSpec(memory_space=pltpu.VMEM)
HBM = pl.BlockSpec(memory_space=pltpu.HBM)


def swap_chan(block):
    return lax.ppermute(block, "chan", [(0, 1), (1, 0)])


def swap_lat(block):
    bands, groups = lax.axis_size("lat"), lax.axis_size("grp")
    last = 2 * bands - 1
    pairs = []
    for group in range(groups):
        for i in range(1, last, 2):
            pairs += [(group, i, group, i + 1), (group, i + 1, group, i)]
        mate = group ^ 1 if group ^ 1 < groups else group
        pairs += [(group, 0, mate, 0), (group, last, mate, last)]
    route = [(g * 2 * bands + i, m * 2 * bands + k) for g, i, m, k in pairs]
    return lax.ppermute(block, ("grp", "lat", "chan"), route)


def to_earlier(block):
    count = lax.axis_size("tm")
    return lax.ppermute(block, "tm", [(i, (i - 1) % count) for i in range(count)])


def lane_shift(values, step):
    lanes = lax.broadcasted_iota(jnp.int32, values.shape, 1)
    edge = 0 if step == 1 else values.shape[1] - 1
    return jnp.where(lanes == edge, 0.0, pltpu.roll(values, step % values.shape[1], 1))


def tile_mask(mask_ref, cells):
    tile = lax.broadcasted_iota(jnp.int32, (1, cells), 1) // 32
    seen = jnp.zeros((1, cells), jnp.float32)
    for t in range(cells // 32):
        seen = jnp.where(tile == t, mask_ref[t].astype(jnp.float32), seen)
    return seen


def split_rows(dims, wide, piece, refs):
    fronts, states, cells = dims
    chan = lax.axis_index("chan")
    for p, ref in enumerate(refs):
        first = 2 * chan if p < fronts // 2 else 2 - 2 * chan
        front = 2 * (p % (fronts // 2))
        for i in range(2):
            for f in range(2):
                rows = wide[pl.ds((front + f) * states * 4 + first + i, states, stride=4), :]
                piece[pl.ds(i * 2 + f, states, stride=4), :] = rows
        ref[...] = piece[...].astype(jnp.bfloat16)


def spread_rows(dims, ref, front, piece, field, start, used):
    states, pitch, cells = dims
    piece[...] = jnp.where(used, ref[:4 * states, :].astype(jnp.float32), 0.0)
    for i in range(2):
        for f in range(2):
            rows = piece[pl.ds(i * 2 + f, states, stride=4), :]
            spot = pl.ds(pl.multiple_of(start + i * pitch, 16), states)
            lanes = slice((front + f) * cells, (front + f + 1) * cells)
            field[spot, lanes] = rows.astype(jnp.bfloat16)


def split_kernel(dims, state_ref, *refs):
    *pieces, wide, piece = refs
    wide[...] = state_ref[...]
    split_rows(dims, wide, piece, pieces)


def first_kernel(
    dims, layer_ref, mask_ref, innov_ref, slope_ref, out_ref, in_ref,
    *refs,
):
    fronts, states, cells, half = dims
    *pieces, forcing_ref, raw_ref = refs[:fronts + 2]
    layers, mask, innov, slope, taps_out, taps_in, wide, piece, sem = refs[fronts + 2:]

    def fetch(i, src, dst):
        copy = pltpu.make_async_copy(src, dst, sem.at[i])
        copy.start()
        return copy

    fetches = [
        fetch(i, src, dst)
        for i, (src, dst) in enumerate(
            ((layer_ref, layers), (mask_ref, mask), (innov_ref, innov), (slope_ref, slope))
        )
    ]
    fetches[0].wait()
    layer = layers[lax.axis_index("tm")]
    fetches += [fetch(4, out_ref.at[layer], taps_out), fetch(5, in_ref.at[layer], taps_in)]
    fetches[1].wait()
    fetches[2].wait()
    wide[...] = innov[...].astype(jnp.float32) * tile_mask(mask, cells)
    split_rows((fronts, states, cells), wide, piece, pieces)
    forcing_ref[...] = wide[...].astype(jnp.bfloat16)
    fetches[3].wait()
    raw_ref[18 * half:, :] = slope[...]
    for i, taps in enumerate((taps_out, taps_in)):
        fetches[4 + i].wait()
        for t in range(9):
            start = (9 * i + t) * half
            raw_ref[start:start + half, :states] = taps[t // 3, t % 3]


def order_kernel(dims, own_ref, away_ref, first_ref, second_ref, slope_ref, edge_ref, wide):
    states, pitch, half, cells = dims
    hidden, lanes = 2 * half, 2 * cells
    chan = lax.axis_index("chan")
    inside = lax.broadcasted_iota(jnp.int32, (half, lanes), 1) < states

    def placed(raw_ref, i, a, b, spot):
        start = (9 * i + 3 * a + b) * half
        block = raw_ref[start:start + half, :].astype(jnp.float32)
        block = jnp.where(inside, jnp.concatenate([block, block], axis=1), 0.0)
        return block if spot == 0 else pltpu.roll(block, spot * pitch, 1)

    turned = [[None, None] for _ in range(3)]
    for part, raw_ref in enumerate((own_ref, away_ref)):
        for b in range(3):
            rows = sum(placed(raw_ref, 0, a, b, 2 - a) for a in range(3))
            start = b * hidden + part * half
            first_ref[start:start + half, :] = rows.astype(jnp.bfloat16)
        for a in range(3):
            turned[2 - a][part] = sum(placed(raw_ref, 1, a, b, b) for b in range(3))
        wide[...] = raw_ref[18 * half:, :].astype(jnp.float32)
        for j in range(6):
            lat_row = jnp.clip(4 * chan + j - 1, 0, 7)
            start = j * hidden + part * half
            slope_ref[start:start + half, :] = wide[pl.ds(lat_row, half, stride=8), :].astype(jnp.bfloat16)
        start = (1 - part) * half
        edge_ref[start:start + half, :] = wide[pl.ds(7 * chan, half, stride=8), :].astype(jnp.bfloat16)
    turned = jnp.concatenate([block for pair in turned for block in pair], axis=0).T
    second_ref[...] = turned[:3 * pitch].astype(jnp.bfloat16)


def hidden_row(dims, j, first_ref, slope, field, hidden_grad, spot):
    fronts, pitch, hidden, cells = dims
    for pair in range(fronts // 2):
        taps = jnp.dot(
            first_ref[:, :3 * pitch],
            field[j * pitch:(j + 3) * pitch, 2 * pair * cells:2 * (pair + 1) * cells],
            preferred_element_type=jnp.float32,
        )
        for f in range(2):
            lanes = slice(f * cells, (f + 1) * cells)
            total = (
                taps[hidden:2 * hidden, lanes]
                + lane_shift(taps[0:hidden, lanes], -1)
                + lane_shift(taps[2 * hidden:3 * hidden, lanes], 1)
            )
            start = (2 * pair + f) * cells
            hidden_grad[spot:spot + hidden, start:start + cells] = (slope * total).astype(jnp.bfloat16)


def join_kernel(join, piece_ref, edge_ref, joined_ref):
    joined_ref[:piece_ref.shape[0], :] = piece_ref[...]
    joined_ref[join:, :] = edge_ref[...]


def own_kernel(dims, *refs):
    fronts, states, pitch, hidden, cells = dims
    pieces = refs[:fronts]
    first_ref, slope_ref, field_ref, hidden_ref, piece = refs[fronts:]
    chan = lax.axis_index("chan")
    live = lax.axis_index("tm") < lax.axis_size("tm") - 1
    field_ref[...] = jnp.zeros_like(field_ref)
    for p, ref in enumerate(pieces):
        start = (chan if p < fronts // 2 else 1 - chan) * 2 * pitch
        front = 2 * (p % (fronts // 2))
        spread_rows((states, pitch, cells), ref, front, piece, field_ref, start, live)
    for j in range(2):
        slope = slope_ref[(j + 2) * hidden:(j + 3) * hidden, :].astype(jnp.float32)
        hidden_row((fronts, pitch, hidden, cells), j, first_ref, slope, field_ref, hidden_ref, j * hidden)


def step_kernel(dims, *refs):
    fronts, states, pitch, hidden, cells = dims
    pieces = refs[:fronts]
    own_ref, middle_ref, forcing_ref, first_ref, second_ref, slope_ref = refs[fronts:fronts + 6]
    result_ref, field, hidden_grad, piece, result, sem = refs[fronts + 6:]
    edge_ref = pieces[fronts // 2 - 1]
    edge = edge_ref.shape[0] - hidden
    chan, band = lax.axis_index("chan"), lax.axis_index("lat")
    rows = 4
    live = lax.axis_index("tm") < lax.axis_size("tm") - 1
    border = (band == 0) & (chan == 0) | (band == lax.axis_size("lat") - 1) & (chan == 1)
    field[...] = jnp.zeros_like(field)
    for p, ref in enumerate(pieces):
        used = live & ~border if p < fronts // 2 else live
        start = (chan if p < fronts // 2 else 1 - chan) * 6 * pitch
        front = 2 * (p % (fronts // 2))
        spread_rows((states, pitch, cells), ref, front, piece, field, start, used)
    field[2 * pitch:6 * pitch, :] = own_ref[...]
    hidden_grad[2 * hidden:4 * hidden, :] = middle_ref[...]
    for j in (0, 1, rows, rows + 1):
        slope = slope_ref[j * hidden:(j + 1) * hidden, :].astype(jnp.float32)
        if j in (0, rows + 1):
            beyond = jnp.where(border, 0.0, edge_ref[edge:, :].astype(jnp.float32))
            slope = jnp.where(chan == (0 if j == 0 else 1), beyond, slope)
        hidden_row((fronts, pitch, hidden, cells), j, first_ref, slope, field, hidden_grad, j * hidden)

    size = 2 * states * rows
    copies = []
    for pair in range(fronts // 2):
        part = slice(pair * size, (pair + 1) * size)
        result[part, :] = forcing_ref[part, :].astype(jnp.float32)
        block = slice(2 * pair * cells, 2 * (pair + 1) * cells)
        for h in range(rows):
            taps = jnp.dot(
                second_ref[...], hidden_grad[h * hidden:(h + 3) * hidden, block],
                preferred_element_type=jnp.float32,
            )
            before = field[(h + 2) * pitch:(h + 3) * pitch, block].astype(jnp.float32)
            for f in range(2):
                lanes = slice(f * cells, (f + 1) * cells)
                total = (
                    before[:, lanes]
                    + taps[pitch:2 * pitch, lanes]
                    + lane_shift(taps[0:pitch, lanes], -1)
                    + lane_shift(taps[2 * pitch:3 * pitch, lanes], 1)
                )
                spots = pl.ds((2 * pair + f) * states * rows + h, states, stride=rows)
                result[spots, :] = result[spots, :] + total[:states]
        copies.append(pltpu.make_async_copy(result.at[part], result_ref.at[part], sem.at[pair]))
        copies[-1].start()
    for copy in copies:
        copy.wait()


def per_device(innovations, obs_mask, slopes, layer_of, weight_in, weight_out):
    fronts, _, states, rows, cells = innovations.shape
    half = slopes.shape[1]
    hidden = 2 * half
    pitch = -(-states // 16) * 16
    owners = lax.axis_size("tm")
    flat = (fronts * states * rows, cells)

    def array(shape, dtype=jnp.bfloat16):
        return jax.ShapeDtypeStruct(shape, dtype)

    pairs = fronts // 2
    pieces = (array((4 * states, cells)),) * fronts
    piece_wide = pltpu.VMEM(pieces[0].shape, jnp.float32)
    join = -(-4 * states // 16) * 16
    field_shape, hidden_shape = (8 * pitch, fronts * cells), (6 * hidden, fronts * cells)
    modest = pltpu.CompilerParams(vmem_limit_bytes=8 << 20)
    *sent, forcing, raw_own = pl.pallas_call(
        functools.partial(first_kernel, (fronts, states, cells, half)),
        out_shape=pieces + (array(flat), array((26 * half, cells))),
        in_specs=[HBM] * 6,
        out_specs=(VMEM,) * (fronts + 2),
        scratch_shapes=[
            pltpu.SMEM(layer_of.shape, jnp.int32),
            pltpu.SMEM(obs_mask.shape[2:], jnp.int32),
            pltpu.VMEM(flat, jnp.bfloat16),
            pltpu.VMEM((8 * half, cells), jnp.bfloat16),
            pltpu.VMEM((3, 3, half, states), jnp.bfloat16),
            pltpu.VMEM((3, 3, half, states), jnp.bfloat16),
            pltpu.VMEM(flat, jnp.float32),
            piece_wide,
            pltpu.SemaphoreType.DMA((6,)),
        ],
        compiler_params=modest,
    )(
        *(
            pltpu.with_memory_space_constraint(argument, pltpu.HBM)
            for argument in (
                layer_of, obs_mask[0, 0], innovations.reshape(flat), slopes.reshape(8 * half, cells),
                weight_out, weight_in.transpose(0, 1, 2, 4, 3),
            )
        )
    )
    outer = [to_earlier(block) for block in sent[:pairs]]
    raw_away = swap_chan(raw_own)
    first, second, slope, edge = pl.pallas_call(
        functools.partial(order_kernel, (states, pitch, half, cells)),
        out_shape=(
            array((3 * hidden, 2 * cells)), array((3 * pitch, 3 * hidden)),
            array((6 * hidden, cells)), array((hidden, cells)),
        ),
        in_specs=[VMEM] * 2,
        out_specs=(VMEM,) * 4,
        scratch_shapes=[pltpu.VMEM((8 * half, cells), jnp.float32)],
        compiler_params=modest,
    )(raw_own, raw_away)
    edge, sent = lax.optimization_barrier((edge, sent))
    inner = [to_earlier(block) for block in sent[pairs:]]

    for hop in range(1, owners):
        if hop > 1:
            sent = pl.pallas_call(
                functools.partial(split_kernel, (fronts, states, cells)),
                out_shape=pieces,
                in_specs=[VMEM],
                out_specs=(VMEM,) * fronts,
                scratch_shapes=[pltpu.VMEM(flat, jnp.float32), piece_wide],
                compiler_params=modest,
            )(result)
            outer = [to_earlier(block) for block in sent[:pairs]]
            inner = [to_earlier(block) for block in sent[pairs:]]
        joined = pl.pallas_call(
            functools.partial(join_kernel, join),
            out_shape=array((join + hidden, cells)),
            in_specs=[VMEM, VMEM],
            out_specs=VMEM,
            compiler_params=modest,
        )(outer[-1], edge)
        halo = [swap_lat(block) for block in outer[:-1] + [joined]]
        other = [swap_chan(block) for block in inner]
        sizes = (fronts, states, pitch, hidden, cells)
        own, middle = pl.pallas_call(
            functools.partial(own_kernel, sizes),
            out_shape=(array((4 * pitch, fronts * cells)), array((2 * hidden, fronts * cells))),
            in_specs=[VMEM] * (fronts + 2),
            out_specs=(VMEM, VMEM),
            scratch_shapes=[piece_wide],
            compiler_params=modest,
        )(*outer, *inner, first, slope)
        result = pl.pallas_call(
            functools.partial(step_kernel, sizes),
            out_shape=array(flat, jnp.float32),
            in_specs=[VMEM] * (fronts + 6),
            out_specs=HBM,
            scratch_shapes=[
                pltpu.VMEM(field_shape, jnp.bfloat16),
                pltpu.VMEM(hidden_shape, jnp.bfloat16),
                piece_wide,
                pltpu.VMEM(flat, jnp.float32),
                pltpu.SemaphoreType.DMA((fronts // 2,)),
            ],
            compiler_params=modest,
        )(*halo, *other, own, middle, forcing, first, second, slope)
    return result.reshape(innovations.shape)


def solution(mesh):
    return jax.shard_map(
        per_device,
        mesh=mesh,
        in_specs=(
            P(None, ("grp", "tm"), None, ("lat", "chan"), None),
            P(("grp", "tm"), ("lat", "chan"), None),
            P(("grp", "tm"), "chan", "lat", None),
            P(),
            P(None, None, None, None, "chan"),
            P(None, None, None, "chan", None),
        ),
        out_specs=P(None, ("grp", "tm"), None, ("lat", "chan"), None),
        check_vma=False,
    )
```

```python
import functools

import jax
import jax.numpy as jnp
from jax import lax
from jax.experimental import pallas as pl
from jax.experimental.pallas import tpu as pltpu
from jax.sharding import PartitionSpec as P

VMEM = pl.BlockSpec(memory_space=pltpu.VMEM)
HBM = pl.BlockSpec(memory_space=pltpu.HBM)


def swap_chan(block):
    return lax.ppermute(block, "chan", [(0, 1), (1, 0)])


def swap_lat(block):
    bands, groups = lax.axis_size("lat"), lax.axis_size("grp")
    last = 2 * bands - 1
    pairs = []
    for group in range(groups):
        for i in range(1, last, 2):
            pairs += [(group, i, group, i + 1), (group, i + 1, group, i)]
        mate = group ^ 1 if group ^ 1 < groups else group
        pairs += [(group, 0, mate, 0), (group, last, mate, last)]
    route = [(g * 2 * bands + i, m * 2 * bands + k) for g, i, m, k in pairs]
    return lax.ppermute(block, ("grp", "lat", "chan"), route)


def to_earlier(block):
    count = lax.axis_size("tm")
    return lax.ppermute(block, "tm", [(i, (i - 1) % count) for i in range(count)])


def lane_shift(values, step):
    lanes = lax.broadcasted_iota(jnp.int32, values.shape, 1)
    edge = 0 if step == 1 else values.shape[1] - 1
    return jnp.where(lanes == edge, 0.0, pltpu.roll(values, step % values.shape[1], 1))


def tile_mask(mask_ref, cells):
    tile = lax.broadcasted_iota(jnp.int32, (1, cells), 1) // 32
    seen = jnp.zeros((1, cells), jnp.float32)
    for t in range(cells // 32):
        seen = jnp.where(tile == t, mask_ref[t].astype(jnp.float32), seen)
    return seen


def split_rows(dims, wide, piece, refs):
    fronts, states, cells = dims
    chan = lax.axis_index("chan")
    for p, ref in enumerate(refs):
        first = 2 * chan if p < fronts // 2 else 2 - 2 * chan
        front = 2 * (p % (fronts // 2))
        for i in range(2):
            for f in range(2):
                rows = wide[pl.ds((front + f) * states * 4 + first + i, states, stride=4), :]
                piece[pl.ds(i * 2 + f, states, stride=4), :] = rows
        ref[...] = piece[...].astype(jnp.bfloat16)


def spread_rows(dims, ref, front, piece, field, start, used):
    states, pitch, cells = dims
    piece[...] = jnp.where(used, ref[:4 * states, :].astype(jnp.float32), 0.0)
    for i in range(2):
        for f in range(2):
            rows = piece[pl.ds(i * 2 + f, states, stride=4), :]
            spot = pl.ds(pl.multiple_of(start + i * pitch, 16), states)
            lanes = slice((front + f) * cells, (front + f + 1) * cells)
            field[spot, lanes] = rows.astype(jnp.bfloat16)


def split_kernel(dims, state_ref, *refs):
    *pieces, wide, piece = refs
    wide[...] = state_ref[...]
    split_rows(dims, wide, piece, pieces)


def first_kernel(
    dims, layer_ref, mask_ref, innov_ref, slope_ref, out_ref, in_ref,
    *refs,
):
    fronts, states, cells, half = dims
    *pieces, forcing_ref, raw_ref = refs[:fronts + 2]
    layers, mask, innov, slope, taps_out, taps_in, wide, piece, sem = refs[fronts + 2:]

    def fetch(i, src, dst):
        copy = pltpu.make_async_copy(src, dst, sem.at[i])
        copy.start()
        return copy

    fetches = [
        fetch(i, src, dst)
        for i, (src, dst) in enumerate(
            ((layer_ref, layers), (mask_ref, mask), (innov_ref, innov), (slope_ref, raw_ref.at[18 * half:]))
        )
    ]
    fetches[0].wait()
    layer = layers[lax.axis_index("tm")]
    for i, (src, dst) in enumerate(((out_ref, taps_out), (in_ref, taps_in))):
        fetches += [fetch(4 + 3 * i + a, src.at[layer, a], dst.at[a]) for a in range(3)]
    fetches[1].wait()
    fetches[2].wait()
    wide[...] = innov[...].astype(jnp.float32) * tile_mask(mask, cells)
    split_rows((fronts, states, cells), wide, piece, pieces)
    forcing_ref[...] = wide[...].astype(jnp.bfloat16)
    fetches[3].wait()
    for i, taps in enumerate((taps_out, taps_in)):
        for t in range(9):
            if t % 3 == 0:
                fetches[4 + 3 * i + t // 3].wait()
            start = (9 * i + t) * half
            raw_ref[start:start + half, :states] = taps[t // 3, t % 3]


def order_kernel(dims, own_ref, away_ref, first_ref, second_ref, slope_ref, edge_ref, wide):
    states, pitch, half, cells = dims
    hidden, lanes = 2 * half, 2 * cells
    chan = lax.axis_index("chan")
    inside = lax.broadcasted_iota(jnp.int32, (half, lanes), 1) < states

    def placed(raw_ref, i, a, b, spot):
        start = (9 * i + 3 * a + b) * half
        block = raw_ref[start:start + half, :].astype(jnp.float32)
        block = jnp.where(inside, jnp.concatenate([block, block], axis=1), 0.0)
        return block if spot == 0 else pltpu.roll(block, spot * pitch, 1)

    turned = [[None, None] for _ in range(3)]
    for part, raw_ref in enumerate((own_ref, away_ref)):
        for b in range(3):
            rows = sum(placed(raw_ref, 0, a, b, 2 - a) for a in range(3))
            start = b * hidden + part * half
            first_ref[start:start + half, :] = rows.astype(jnp.bfloat16)
        for a in range(3):
            turned[2 - a][part] = sum(placed(raw_ref, 1, a, b, b) for b in range(3))
        wide[...] = raw_ref[18 * half:, :].astype(jnp.float32)
        for j in range(6):
            lat_row = jnp.clip(4 * chan + j - 1, 0, 7)
            start = j * hidden + part * half
            slope_ref[start:start + half, :] = wide[pl.ds(lat_row, half, stride=8), :].astype(jnp.bfloat16)
        start = (1 - part) * half
        edge_ref[start:start + half, :] = wide[pl.ds(7 * chan, half, stride=8), :].astype(jnp.bfloat16)
    turned = jnp.concatenate([block for pair in turned for block in pair], axis=0).T
    second_ref[...] = turned[:3 * pitch].astype(jnp.bfloat16)


def hidden_row(dims, j, first_ref, slope, field, hidden_grad, spot):
    fronts, pitch, hidden, cells = dims
    for pair in range(fronts // 2):
        taps = jnp.dot(
            first_ref[:, :3 * pitch],
            field[j * pitch:(j + 3) * pitch, 2 * pair * cells:2 * (pair + 1) * cells],
            preferred_element_type=jnp.float32,
        )
        for f in range(2):
            lanes = slice(f * cells, (f + 1) * cells)
            total = (
                taps[hidden:2 * hidden, lanes]
                + lane_shift(taps[0:hidden, lanes], -1)
                + lane_shift(taps[2 * hidden:3 * hidden, lanes], 1)
            )
            start = (2 * pair + f) * cells
            hidden_grad[spot:spot + hidden, start:start + cells] = (slope * total).astype(jnp.bfloat16)


def join_kernel(join, piece_ref, edge_ref, joined_ref):
    joined_ref[:piece_ref.shape[0], :] = piece_ref[...]
    joined_ref[join:, :] = edge_ref[...]


def own_kernel(dims, *refs):
    fronts, states, pitch, hidden, cells = dims
    pieces = refs[:fronts]
    first_ref, slope_ref, field_ref, hidden_ref, piece = refs[fronts:]
    chan = lax.axis_index("chan")
    live = lax.axis_index("tm") < lax.axis_size("tm") - 1
    field_ref[...] = jnp.zeros_like(field_ref)
    for p, ref in enumerate(pieces):
        start = (chan if p < fronts // 2 else 1 - chan) * 2 * pitch
        front = 2 * (p % (fronts // 2))
        spread_rows((states, pitch, cells), ref, front, piece, field_ref, start, live)
    for j in range(2):
        slope = slope_ref[(j + 2) * hidden:(j + 3) * hidden, :].astype(jnp.float32)
        hidden_row((fronts, pitch, hidden, cells), j, first_ref, slope, field_ref, hidden_ref, j * hidden)


def step_kernel(dims, *refs):
    fronts, states, pitch, hidden, cells = dims
    pieces = refs[:fronts]
    own_ref, middle_ref, forcing_ref, first_ref, second_ref, slope_ref = refs[fronts:fronts + 6]
    result_ref, field, hidden_grad, piece, result, sem = refs[fronts + 6:]
    edge_ref = pieces[fronts // 2 - 1]
    edge = edge_ref.shape[0] - hidden
    chan, band = lax.axis_index("chan"), lax.axis_index("lat")
    rows = 4
    live = lax.axis_index("tm") < lax.axis_size("tm") - 1
    border = (band == 0) & (chan == 0) | (band == lax.axis_size("lat") - 1) & (chan == 1)
    field[...] = jnp.zeros_like(field)
    for p, ref in enumerate(pieces):
        used = live & ~border if p < fronts // 2 else live
        start = (chan if p < fronts // 2 else 1 - chan) * 6 * pitch
        front = 2 * (p % (fronts // 2))
        spread_rows((states, pitch, cells), ref, front, piece, field, start, used)
    field[2 * pitch:6 * pitch, :] = own_ref[...]
    hidden_grad[2 * hidden:4 * hidden, :] = middle_ref[...]
    for j in (0, 1, rows, rows + 1):
        slope = slope_ref[j * hidden:(j + 1) * hidden, :].astype(jnp.float32)
        if j in (0, rows + 1):
            beyond = jnp.where(border, 0.0, edge_ref[edge:, :].astype(jnp.float32))
            slope = jnp.where(chan == (0 if j == 0 else 1), beyond, slope)
        hidden_row((fronts, pitch, hidden, cells), j, first_ref, slope, field, hidden_grad, j * hidden)

    size = 2 * states * rows
    copies = []
    for pair in range(fronts // 2):
        part = slice(pair * size, (pair + 1) * size)
        result[part, :] = forcing_ref[part, :].astype(jnp.float32)
        block = slice(2 * pair * cells, 2 * (pair + 1) * cells)
        for h in range(rows):
            taps = jnp.dot(
                second_ref[...], hidden_grad[h * hidden:(h + 3) * hidden, block],
                preferred_element_type=jnp.float32,
            )
            before = field[(h + 2) * pitch:(h + 3) * pitch, block].astype(jnp.float32)
            for f in range(2):
                lanes = slice(f * cells, (f + 1) * cells)
                total = (
                    before[:, lanes]
                    + taps[pitch:2 * pitch, lanes]
                    + lane_shift(taps[0:pitch, lanes], -1)
                    + lane_shift(taps[2 * pitch:3 * pitch, lanes], 1)
                )
                spots = pl.ds((2 * pair + f) * states * rows + h, states, stride=rows)
                result[spots, :] = result[spots, :] + total[:states]
        copies.append(pltpu.make_async_copy(result.at[part], result_ref.at[part], sem.at[pair]))
        copies[-1].start()
    for copy in copies:
        copy.wait()


def per_device(innovations, obs_mask, slopes, layer_of, weight_in, weight_out):
    fronts, _, states, rows, cells = innovations.shape
    half = slopes.shape[1]
    hidden = 2 * half
    pitch = -(-states // 16) * 16
    owners = lax.axis_size("tm")
    flat = (fronts * states * rows, cells)

    def array(shape, dtype=jnp.bfloat16):
        return jax.ShapeDtypeStruct(shape, dtype)

    pairs = fronts // 2
    pieces = (array((4 * states, cells)),) * fronts
    piece_wide = pltpu.VMEM(pieces[0].shape, jnp.float32)
    join = -(-4 * states // 16) * 16
    field_shape, hidden_shape = (8 * pitch, fronts * cells), (6 * hidden, fronts * cells)
    modest = pltpu.CompilerParams(vmem_limit_bytes=8 << 20)
    *sent, forcing, raw_own = pl.pallas_call(
        functools.partial(first_kernel, (fronts, states, cells, half)),
        out_shape=pieces + (array(flat), array((26 * half, cells))),
        in_specs=[HBM] * 6,
        out_specs=(VMEM,) * (fronts + 2),
        scratch_shapes=[
            pltpu.SMEM(layer_of.shape, jnp.int32),
            pltpu.SMEM(obs_mask.shape[2:], jnp.int32),
            pltpu.VMEM(flat, jnp.bfloat16),
            pltpu.VMEM((8 * half, cells), jnp.bfloat16),
            pltpu.VMEM((3, 3, half, states), jnp.bfloat16),
            pltpu.VMEM((3, 3, half, states), jnp.bfloat16),
            pltpu.VMEM(flat, jnp.float32),
            piece_wide,
            pltpu.SemaphoreType.DMA((10,)),
        ],
        compiler_params=modest,
    )(
        *(
            pltpu.with_memory_space_constraint(argument, pltpu.HBM)
            for argument in (
                layer_of, obs_mask[0, 0], innovations.reshape(flat), slopes.reshape(8 * half, cells),
                weight_out, weight_in.transpose(0, 1, 2, 4, 3),
            )
        )
    )
    outer = [to_earlier(block) for block in sent[:pairs]]
    raw_away = swap_chan(raw_own)
    first, second, slope, edge = pl.pallas_call(
        functools.partial(order_kernel, (states, pitch, half, cells)),
        out_shape=(
            array((3 * hidden, 2 * cells)), array((3 * pitch, 3 * hidden)),
            array((6 * hidden, cells)), array((hidden, cells)),
        ),
        in_specs=[VMEM] * 2,
        out_specs=(VMEM,) * 4,
        scratch_shapes=[pltpu.VMEM((8 * half, cells), jnp.float32)],
        compiler_params=modest,
    )(raw_own, raw_away)
    inner = [to_earlier(block) for block in sent[pairs:]]

    for hop in range(1, owners):
        if hop > 1:
            sent = pl.pallas_call(
                functools.partial(split_kernel, (fronts, states, cells)),
                out_shape=pieces,
                in_specs=[VMEM],
                out_specs=(VMEM,) * fronts,
                scratch_shapes=[pltpu.VMEM(flat, jnp.float32), piece_wide],
                compiler_params=modest,
            )(result)
            outer = [to_earlier(block) for block in sent[:pairs]]
            inner = [to_earlier(block) for block in sent[pairs:]]
        joined = pl.pallas_call(
            functools.partial(join_kernel, join),
            out_shape=array((join + hidden, cells)),
            in_specs=[VMEM, VMEM],
            out_specs=VMEM,
            compiler_params=modest,
        )(outer[-1], edge)
        halo = [swap_lat(block) for block in outer[:-1] + [joined]]
        other = [swap_chan(block) for block in inner]
        sizes = (fronts, states, pitch, hidden, cells)
        own, middle = pl.pallas_call(
            functools.partial(own_kernel, sizes),
            out_shape=(array((4 * pitch, fronts * cells)), array((2 * hidden, fronts * cells))),
            in_specs=[VMEM] * (fronts + 2),
            out_specs=(VMEM, VMEM),
            scratch_shapes=[piece_wide],
            compiler_params=modest,
        )(*outer, *inner, first, slope)
        result = pl.pallas_call(
            functools.partial(step_kernel, sizes),
            out_shape=array(flat, jnp.float32),
            in_specs=[VMEM] * (fronts + 6),
            out_specs=HBM,
            scratch_shapes=[
                pltpu.VMEM(field_shape, jnp.bfloat16),
                pltpu.VMEM(hidden_shape, jnp.bfloat16),
                piece_wide,
                pltpu.VMEM(flat, jnp.float32),
                pltpu.SemaphoreType.DMA((fronts // 2,)),
            ],
            compiler_params=modest,
        )(*halo, *other, own, middle, forcing, first, second, slope)
    return result.reshape(innovations.shape)


def solution(mesh):
    return jax.shard_map(
        per_device,
        mesh=mesh,
        in_specs=(
            P(None, ("grp", "tm"), None, ("lat", "chan"), None),
            P(("grp", "tm"), ("lat", "chan"), None),
            P(("grp", "tm"), "chan", "lat", None),
            P(),
            P(None, None, None, None, "chan"),
            P(None, None, None, "chan", None),
        ),
        out_specs=P(None, ("grp", "tm"), None, ("lat", "chan"), None),
        check_vma=False,
    )
```

```python
import functools

import jax
import jax.numpy as jnp
from jax import lax
from jax.experimental import pallas as pl
from jax.experimental.pallas import tpu as pltpu
from jax.sharding import PartitionSpec as P

VMEM = pl.BlockSpec(memory_space=pltpu.VMEM)
HBM = pl.BlockSpec(memory_space=pltpu.HBM)


def swap_chan(block):
    return lax.ppermute(block, "chan", [(0, 1), (1, 0)])


def swap_lat(block):
    bands, groups = lax.axis_size("lat"), lax.axis_size("grp")
    last = 2 * bands - 1
    pairs = []
    for group in range(groups):
        for i in range(1, last, 2):
            pairs += [(group, i, group, i + 1), (group, i + 1, group, i)]
        mate = group ^ 1 if group ^ 1 < groups else group
        pairs += [(group, 0, mate, 0), (group, last, mate, last)]
    route = [(g * 2 * bands + i, m * 2 * bands + k) for g, i, m, k in pairs]
    return lax.ppermute(block, ("grp", "lat", "chan"), route)


def to_earlier(block):
    count = lax.axis_size("tm")
    return lax.ppermute(block, "tm", [(i, (i - 1) % count) for i in range(count)])


def lane_shift(values, step):
    lanes = lax.broadcasted_iota(jnp.int32, values.shape, 1)
    edge = 0 if step == 1 else values.shape[1] - 1
    return jnp.where(lanes == edge, 0.0, pltpu.roll(values, step % values.shape[1], 1))


def tile_mask(mask_ref, cells):
    tile = lax.broadcasted_iota(jnp.int32, (1, cells), 1) // 32
    seen = jnp.zeros((1, cells), jnp.float32)
    for t in range(cells // 32):
        seen = jnp.where(tile == t, mask_ref[t].astype(jnp.float32), seen)
    return seen


def split_rows(dims, wide, piece, refs):
    fronts, states, cells = dims
    chan = lax.axis_index("chan")
    for p, ref in enumerate(refs):
        first = 2 * chan if p < fronts // 2 else 2 - 2 * chan
        front = 2 * (p % (fronts // 2))
        for i in range(2):
            for f in range(2):
                rows = wide[pl.ds((front + f) * states * 4 + first + i, states, stride=4), :]
                piece[pl.ds(i * 2 + f, states, stride=4), :] = rows
        ref[...] = piece[...].astype(jnp.bfloat16)


def spread_rows(dims, ref, front, piece, field, start, used):
    states, pitch, cells = dims
    piece[...] = jnp.where(used, ref[:4 * states, :].astype(jnp.float32), 0.0)
    for i in range(2):
        for f in range(2):
            rows = piece[pl.ds(i * 2 + f, states, stride=4), :]
            spot = pl.ds(pl.multiple_of(start + i * pitch, 16), states)
            lanes = slice((front + f) * cells, (front + f + 1) * cells)
            field[spot, lanes] = rows.astype(jnp.bfloat16)


def outside_grid():
    chan, band = lax.axis_index("chan"), lax.axis_index("lat")
    return (band == 0) & (chan == 0) | (band == lax.axis_size("lat") - 1) & (chan == 1)


def split_kernel(dims, state_ref, *refs):
    *pieces, wide, piece = refs
    wide[...] = state_ref[...]
    split_rows(dims, wide, piece, pieces)


def first_kernel(
    dims, layer_ref, mask_ref, innov_ref, slope_ref, out_ref, in_ref,
    *refs,
):
    fronts, states, cells, half = dims
    *pieces, forcing_ref, raw_ref = refs[:fronts + 2]
    layers, mask, innov, slope, taps_out, taps_in, wide, piece, sem = refs[fronts + 2:]

    def fetch(i, src, dst):
        copy = pltpu.make_async_copy(src, dst, sem.at[i])
        copy.start()
        return copy

    fetches = [
        fetch(i, src, dst)
        for i, (src, dst) in enumerate(
            ((layer_ref, layers), (mask_ref, mask), (innov_ref, innov), (slope_ref, raw_ref.at[18 * half:]))
        )
    ]
    fetches[0].wait()
    layer = layers[lax.axis_index("tm")]
    for i, (src, dst) in enumerate(((out_ref, taps_out), (in_ref, taps_in))):
        fetches += [fetch(4 + 3 * i + a, src.at[layer, a], dst.at[a]) for a in range(3)]
    fetches[1].wait()
    fetches[2].wait()
    wide[...] = innov[...].astype(jnp.float32) * tile_mask(mask, cells)
    split_rows((fronts, states, cells), wide, piece, pieces)
    forcing_ref[...] = wide[...].astype(jnp.bfloat16)
    fetches[3].wait()
    for i, taps in enumerate((taps_out, taps_in)):
        for t in range(9):
            if t % 3 == 0:
                fetches[4 + 3 * i + t // 3].wait()
            start = (9 * i + t) * half
            raw_ref[start:start + half, :states] = taps[t // 3, t % 3]


def order_kernel(dims, own_ref, away_ref, first_ref, second_ref, slope_ref, edge_ref, wide):
    states, pitch, half, cells = dims
    hidden, lanes = 2 * half, 2 * cells
    chan = lax.axis_index("chan")
    inside = lax.broadcasted_iota(jnp.int32, (half, lanes), 1) < states

    def placed(raw_ref, i, a, b, spot):
        start = (9 * i + 3 * a + b) * half
        block = raw_ref[start:start + half, :].astype(jnp.float32)
        block = jnp.where(inside, jnp.concatenate([block, block], axis=1), 0.0)
        return block if spot == 0 else pltpu.roll(block, spot * pitch, 1)

    turned = [[None, None] for _ in range(3)]
    for part, raw_ref in enumerate((own_ref, away_ref)):
        for b in range(3):
            rows = sum(placed(raw_ref, 0, a, b, 2 - a) for a in range(3))
            start = b * hidden + part * half
            first_ref[start:start + half, :] = rows.astype(jnp.bfloat16)
        for a in range(3):
            turned[2 - a][part] = sum(placed(raw_ref, 1, a, b, b) for b in range(3))
        wide[...] = raw_ref[18 * half:, :].astype(jnp.float32)
        for j in range(6):
            lat_row = jnp.clip(4 * chan + j - 1, 0, 7)
            start = j * hidden + part * half
            slope_ref[start:start + half, :] = wide[pl.ds(lat_row, half, stride=8), :].astype(jnp.bfloat16)
        start = (1 - part) * half
        edge_ref[start:start + half, :] = wide[pl.ds(7 * chan, half, stride=8), :].astype(jnp.bfloat16)
    turned = jnp.concatenate([block for pair in turned for block in pair], axis=0).T
    second_ref[...] = turned[:3 * pitch].astype(jnp.bfloat16)


def hidden_row(dims, j, first_ref, slope, field, hidden_grad, pairs):
    fronts, pitch, hidden, cells = dims
    near = pl.ds(pl.multiple_of(j * pitch, 16), 3 * pitch)
    spot = pl.ds(pl.multiple_of(j * hidden, 16), hidden)
    for pair in pairs:
        taps = jnp.dot(
            first_ref[:, :3 * pitch],
            field[near, 2 * pair * cells:2 * (pair + 1) * cells],
            preferred_element_type=jnp.float32,
        )
        for f in range(2):
            lanes = slice(f * cells, (f + 1) * cells)
            total = (
                taps[hidden:2 * hidden, lanes]
                + lane_shift(taps[0:hidden, lanes], -1)
                + lane_shift(taps[2 * hidden:3 * hidden, lanes], 1)
            )
            start = (2 * pair + f) * cells
            hidden_grad[spot, start:start + cells] = (slope * total).astype(jnp.bfloat16)


def join_kernel(join, piece_ref, edge_ref, joined_ref):
    joined_ref[:piece_ref.shape[0], :] = piece_ref[...]
    joined_ref[join:, :] = edge_ref[...]


def own_kernel(dims, *refs):
    fronts, states, pitch, hidden, cells = dims
    pieces = refs[:fronts]
    halo_ref, first_ref, slope_ref, field_ref, hidden_ref, piece = refs[fronts:]
    sizes = (fronts, pitch, hidden, cells)
    chan = lax.axis_index("chan")
    live = lax.axis_index("tm") < lax.axis_size("tm") - 1
    field_ref[...] = jnp.zeros_like(field_ref)
    for p, ref in enumerate(pieces):
        start = ((chan if p < fronts // 2 else 1 - chan) + 1) * 2 * pitch
        front = 2 * (p % (fronts // 2))
        spread_rows((states, pitch, cells), ref, front, piece, field_ref, start, live)
    for j in (2, 3):
        slope = slope_ref[j * hidden:(j + 1) * hidden, :].astype(jnp.float32)
        hidden_row(sizes, j, first_ref, slope, field_ref, hidden_ref, range(fronts // 2))
    pair = fronts // 2 - 1
    outside = outside_grid()
    spread_rows(
        (states, pitch, cells), halo_ref, 2 * pair, piece, field_ref, chan * 6 * pitch, live & ~outside
    )
    edge = halo_ref[halo_ref.shape[0] - hidden:, :].astype(jnp.float32)
    for i in range(2):
        j = 4 * chan + i
        slope = slope_ref[pl.ds(pl.multiple_of(j * hidden, 16), hidden), :].astype(jnp.float32)
        slope = jnp.where(chan == i, jnp.where(outside, 0.0, edge), slope)
        hidden_row(sizes, j, first_ref, slope, field_ref, hidden_ref, (pair,))


def step_kernel(dims, *refs):
    fronts, states, pitch, hidden, cells = dims
    pieces = refs[:fronts]
    _, _, forcing_ref, first_ref, second_ref, slope_ref = refs[fronts:fronts + 6]
    result_ref, field, hidden_grad, piece, result, sem = refs[fronts + 6:]
    edge_ref = pieces[fronts // 2 - 1]
    edge = edge_ref.shape[0] - hidden
    chan = lax.axis_index("chan")
    rows = 4
    sizes = (fronts, pitch, hidden, cells)
    live = lax.axis_index("tm") < lax.axis_size("tm") - 1
    border = outside_grid()
    for p, ref in enumerate(pieces):
        if p == fronts // 2 - 1:
            continue
        used = live & ~border if p < fronts // 2 else live
        start = (chan if p < fronts // 2 else 1 - chan) * 6 * pitch
        front = 2 * (p % (fronts // 2))
        spread_rows((states, pitch, cells), ref, front, piece, field, start, used)
    for j in (0, 1, rows, rows + 1):
        slope = slope_ref[j * hidden:(j + 1) * hidden, :].astype(jnp.float32)
        if j in (0, rows + 1):
            beyond = jnp.where(border, 0.0, edge_ref[edge:, :].astype(jnp.float32))
            slope = jnp.where(chan == (0 if j == 0 else 1), beyond, slope)
        hidden_row(sizes, j, first_ref, slope, field, hidden_grad, range(fronts // 2 - 1))
    for i in range(2):
        j = 4 * (1 - chan) + i
        slope = slope_ref[pl.ds(pl.multiple_of(j * hidden, 16), hidden), :].astype(jnp.float32)
        hidden_row(sizes, j, first_ref, slope, field, hidden_grad, (fronts // 2 - 1,))

    size = 2 * states * rows
    copies = []
    for pair in range(fronts // 2):
        part = slice(pair * size, (pair + 1) * size)
        result[part, :] = forcing_ref[part, :].astype(jnp.float32)
        block = slice(2 * pair * cells, 2 * (pair + 1) * cells)
        for h in range(rows):
            taps = jnp.dot(
                second_ref[...], hidden_grad[h * hidden:(h + 3) * hidden, block],
                preferred_element_type=jnp.float32,
            )
            before = field[(h + 2) * pitch:(h + 3) * pitch, block].astype(jnp.float32)
            for f in range(2):
                lanes = slice(f * cells, (f + 1) * cells)
                total = (
                    before[:, lanes]
                    + taps[pitch:2 * pitch, lanes]
                    + lane_shift(taps[0:pitch, lanes], -1)
                    + lane_shift(taps[2 * pitch:3 * pitch, lanes], 1)
                )
                spots = pl.ds((2 * pair + f) * states * rows + h, states, stride=rows)
                result[spots, :] = result[spots, :] + total[:states]
        copies.append(pltpu.make_async_copy(result.at[part], result_ref.at[part], sem.at[pair]))
        copies[-1].start()
    for copy in copies:
        copy.wait()


def per_device(innovations, obs_mask, slopes, layer_of, weight_in, weight_out):
    fronts, _, states, rows, cells = innovations.shape
    half = slopes.shape[1]
    hidden = 2 * half
    pitch = -(-states // 16) * 16
    owners = lax.axis_size("tm")
    flat = (fronts * states * rows, cells)

    def array(shape, dtype=jnp.bfloat16):
        return jax.ShapeDtypeStruct(shape, dtype)

    pairs = fronts // 2
    pieces = (array((4 * states, cells)),) * fronts
    piece_wide = pltpu.VMEM(pieces[0].shape, jnp.float32)
    join = -(-4 * states // 16) * 16
    field_shape, hidden_shape = (8 * pitch, fronts * cells), (6 * hidden, fronts * cells)
    modest = pltpu.CompilerParams(vmem_limit_bytes=8 << 20)
    *sent, forcing, raw_own = pl.pallas_call(
        functools.partial(first_kernel, (fronts, states, cells, half)),
        out_shape=pieces + (array(flat), array((26 * half, cells))),
        in_specs=[HBM] * 6,
        out_specs=(VMEM,) * (fronts + 2),
        scratch_shapes=[
            pltpu.SMEM(layer_of.shape, jnp.int32),
            pltpu.SMEM(obs_mask.shape[2:], jnp.int32),
            pltpu.VMEM(flat, jnp.bfloat16),
            pltpu.VMEM((8 * half, cells), jnp.bfloat16),
            pltpu.VMEM((3, 3, half, states), jnp.bfloat16),
            pltpu.VMEM((3, 3, half, states), jnp.bfloat16),
            pltpu.VMEM(flat, jnp.float32),
            piece_wide,
            pltpu.SemaphoreType.DMA((10,)),
        ],
        compiler_params=modest,
    )(
        *(
            pltpu.with_memory_space_constraint(argument, pltpu.HBM)
            for argument in (
                layer_of, obs_mask[0, 0], innovations.reshape(flat), slopes.reshape(8 * half, cells),
                weight_out, weight_in.transpose(0, 1, 2, 4, 3),
            )
        )
    )
    outer = [to_earlier(block) for block in sent[:pairs]]
    raw_away = swap_chan(raw_own)
    first, second, slope, edge = pl.pallas_call(
        functools.partial(order_kernel, (states, pitch, half, cells)),
        out_shape=(
            array((3 * hidden, 2 * cells)), array((3 * pitch, 3 * hidden)),
            array((6 * hidden, cells)), array((hidden, cells)),
        ),
        in_specs=[VMEM] * 2,
        out_specs=(VMEM,) * 4,
        scratch_shapes=[pltpu.VMEM((8 * half, cells), jnp.float32)],
        compiler_params=modest,
    )(raw_own, raw_away)
    inner = [to_earlier(block) for block in sent[pairs:]]

    for hop in range(1, owners):
        if hop > 1:
            sent = pl.pallas_call(
                functools.partial(split_kernel, (fronts, states, cells)),
                out_shape=pieces,
                in_specs=[VMEM],
                out_specs=(VMEM,) * fronts,
                scratch_shapes=[pltpu.VMEM(flat, jnp.float32), piece_wide],
                compiler_params=modest,
            )(result)
            outer = [to_earlier(block) for block in sent[:pairs]]
            inner = [to_earlier(block) for block in sent[pairs:]]
        joined = pl.pallas_call(
            functools.partial(join_kernel, join),
            out_shape=array((join + hidden, cells)),
            in_specs=[VMEM, VMEM],
            out_specs=VMEM,
            compiler_params=modest,
        )(outer[-1], edge)
        halo = [swap_lat(block) for block in outer[:-1] + [joined]]
        other = [swap_chan(block) for block in inner]
        sizes = (fronts, states, pitch, hidden, cells)
        own, middle = pl.pallas_call(
            functools.partial(own_kernel, sizes),
            out_shape=(array(field_shape), array(hidden_shape)),
            in_specs=[VMEM] * (fronts + 3),
            out_specs=(VMEM, VMEM),
            scratch_shapes=[piece_wide],
            compiler_params=modest,
        )(*outer, *inner, halo[-1], first, slope)
        result, _, _ = pl.pallas_call(
            functools.partial(step_kernel, sizes),
            out_shape=(array(flat, jnp.float32), array(field_shape), array(hidden_shape)),
            in_specs=[VMEM] * (fronts + 6),
            out_specs=(HBM, VMEM, VMEM),
            input_output_aliases={fronts: 1, fronts + 1: 2},
            scratch_shapes=[
                piece_wide,
                pltpu.VMEM(flat, jnp.float32),
                pltpu.SemaphoreType.DMA((fronts // 2,)),
            ],
            compiler_params=modest,
        )(*halo, *other, own, middle, forcing, first, second, slope)
    return result.reshape(innovations.shape)


def solution(mesh):
    return jax.shard_map(
        per_device,
        mesh=mesh,
        in_specs=(
            P(None, ("grp", "tm"), None, ("lat", "chan"), None),
            P(("grp", "tm"), ("lat", "chan"), None),
            P(("grp", "tm"), "chan", "lat", None),
            P(),
            P(None, None, None, None, "chan"),
            P(None, None, None, "chan", None),
        ),
        out_specs=P(None, ("grp", "tm"), None, ("lat", "chan"), None),
        check_vma=False,
    )
```

```python
import functools

import jax
import jax.numpy as jnp
from jax import lax
from jax.experimental import pallas as pl
from jax.experimental.pallas import tpu as pltpu
from jax.sharding import PartitionSpec as P

VMEM = pl.BlockSpec(memory_space=pltpu.VMEM)
HBM = pl.BlockSpec(memory_space=pltpu.HBM)


def swap_chan(block):
    return lax.ppermute(block, "chan", [(0, 1), (1, 0)])


def swap_lat(block):
    bands, groups = lax.axis_size("lat"), lax.axis_size("grp")
    last = 2 * bands - 1
    pairs = []
    for group in range(groups):
        for i in range(1, last, 2):
            pairs += [(group, i, group, i + 1), (group, i + 1, group, i)]
        mate = group ^ 1 if group ^ 1 < groups else group
        pairs += [(group, 0, mate, 0), (group, last, mate, last)]
    route = [(g * 2 * bands + i, m * 2 * bands + k) for g, i, m, k in pairs]
    return lax.ppermute(block, ("grp", "lat", "chan"), route)


def to_earlier(block):
    count = lax.axis_size("tm")
    return lax.ppermute(block, "tm", [(i, (i - 1) % count) for i in range(count)])


def lane_shift(values, step):
    lanes = lax.broadcasted_iota(jnp.int32, values.shape, 1)
    edge = 0 if step == 1 else values.shape[1] - 1
    return jnp.where(lanes == edge, 0.0, pltpu.roll(values, step % values.shape[1], 1))


def tile_mask(mask_ref, cells):
    tile = lax.broadcasted_iota(jnp.int32, (1, cells), 1) // 32
    seen = jnp.zeros((1, cells), jnp.float32)
    for t in range(cells // 32):
        seen = jnp.where(tile == t, mask_ref[t].astype(jnp.float32), seen)
    return seen


def split_rows(dims, wide, piece, refs):
    fronts, states, cells = dims
    chan = lax.axis_index("chan")
    for p, ref in enumerate(refs):
        first = 2 * chan if p < fronts // 2 else 2 - 2 * chan
        front = 2 * (p % (fronts // 2))
        for i in range(2):
            for f in range(2):
                rows = wide[pl.ds((front + f) * states * 4 + first + i, states, stride=4), :]
                piece[pl.ds(i * 2 + f, states, stride=4), :] = rows
        ref[...] = piece[...].astype(jnp.bfloat16)


def spread_rows(dims, ref, front, piece, field, start, used):
    states, pitch, cells = dims
    piece[...] = jnp.where(used, ref[:4 * states, :].astype(jnp.float32), 0.0)
    for i in range(2):
        for f in range(2):
            rows = piece[pl.ds(i * 2 + f, states, stride=4), :]
            spot = pl.ds(pl.multiple_of(start + i * pitch, 16), states)
            lanes = slice((front + f) * cells, (front + f + 1) * cells)
            field[spot, lanes] = rows.astype(jnp.bfloat16)


def outside_grid():
    chan, band = lax.axis_index("chan"), lax.axis_index("lat")
    return (band == 0) & (chan == 0) | (band == lax.axis_size("lat") - 1) & (chan == 1)


def split_kernel(dims, state_ref, *refs):
    *pieces, wide, piece = refs
    wide[...] = state_ref[...]
    split_rows(dims, wide, piece, pieces)


def first_kernel(
    dims, layer_ref, mask_ref, innov_ref, slope_ref, out_ref, in_ref,
    *refs,
):
    fronts, states, cells, half = dims
    *pieces, forcing_ref, raw_ref = refs[:fronts + 2]
    layers, mask, innov, slope, taps_out, taps_in, wide, piece, sem = refs[fronts + 2:]

    def fetch(i, src, dst):
        copy = pltpu.make_async_copy(src, dst, sem.at[i])
        copy.start()
        return copy

    fetches = [
        fetch(i, src, dst)
        for i, (src, dst) in enumerate(
            ((layer_ref, layers), (mask_ref, mask), (innov_ref, innov), (slope_ref, raw_ref.at[18 * half:]))
        )
    ]
    fetches[0].wait()
    layer = layers[lax.axis_index("tm")]
    for i, (src, dst) in enumerate(((out_ref, taps_out), (in_ref, taps_in))):
        fetches += [fetch(4 + 3 * i + a, src.at[layer, a], dst.at[a]) for a in range(3)]
    fetches[1].wait()
    fetches[2].wait()
    wide[...] = innov[...].astype(jnp.float32) * tile_mask(mask, cells)
    split_rows((fronts, states, cells), wide, piece, pieces)
    forcing_ref[...] = wide[...].astype(jnp.bfloat16)
    fetches[3].wait()
    for i, taps in enumerate((taps_out, taps_in)):
        for t in range(9):
            if t % 3 == 0:
                fetches[4 + 3 * i + t // 3].wait()
            start = (9 * i + t) * half
            raw_ref[start:start + half, :states] = taps[t // 3, t % 3]


def order_kernel(dims, own_ref, away_ref, first_ref, second_ref, slope_ref, edge_ref, wide):
    states, pitch, half, cells = dims
    hidden, lanes = 2 * half, 2 * cells
    chan = lax.axis_index("chan")
    inside = lax.broadcasted_iota(jnp.int32, (half, lanes), 1) < states

    def placed(raw_ref, i, a, b, spot):
        start = (9 * i + 3 * a + b) * half
        block = raw_ref[start:start + half, :].astype(jnp.float32)
        block = jnp.where(inside, jnp.concatenate([block, block], axis=1), 0.0)
        return block if spot == 0 else pltpu.roll(block, spot * pitch, 1)

    turned = [[None, None] for _ in range(3)]
    for part, raw_ref in enumerate((own_ref, away_ref)):
        for b in range(3):
            rows = sum(placed(raw_ref, 0, a, b, 2 - a) for a in range(3))
            start = b * hidden + part * half
            first_ref[start:start + half, :] = rows.astype(jnp.bfloat16)
        for a in range(3):
            turned[2 - a][part] = sum(placed(raw_ref, 1, a, b, b) for b in range(3))
        wide[...] = raw_ref[18 * half:, :].astype(jnp.float32)
        for j in range(6):
            lat_row = jnp.clip(4 * chan + j - 1, 0, 7)
            start = j * hidden + part * half
            slope_ref[start:start + half, :] = wide[pl.ds(lat_row, half, stride=8), :].astype(jnp.bfloat16)
        start = (1 - part) * half
        edge_ref[start:start + half, :] = wide[pl.ds(7 * chan, half, stride=8), :].astype(jnp.bfloat16)
    turned = jnp.concatenate([block for pair in turned for block in pair], axis=0).T
    second_ref[...] = turned[:3 * pitch].astype(jnp.bfloat16)


def hidden_row(dims, j, first_ref, slope, field, hidden_grad, pairs):
    fronts, pitch, hidden, cells = dims
    near = pl.ds(pl.multiple_of(j * pitch, 16), 3 * pitch)
    spot = pl.ds(pl.multiple_of(j * hidden, 16), hidden)
    for pair in pairs:
        taps = jnp.dot(
            first_ref[:, :3 * pitch],
            field[near, 2 * pair * cells:2 * (pair + 1) * cells],
            preferred_element_type=jnp.float32,
        )
        for f in range(2):
            lanes = slice(f * cells, (f + 1) * cells)
            total = (
                taps[hidden:2 * hidden, lanes]
                + lane_shift(taps[0:hidden, lanes], -1)
                + lane_shift(taps[2 * hidden:3 * hidden, lanes], 1)
            )
            start = (2 * pair + f) * cells
            hidden_grad[spot, start:start + cells] = (slope * total).astype(jnp.bfloat16)


def join_kernel(join, piece_ref, edge_ref, joined_ref):
    joined_ref[:piece_ref.shape[0], :] = piece_ref[...]
    joined_ref[join:, :] = edge_ref[...]


def own_kernel(dims, *refs):
    fronts, states, pitch, hidden, cells = dims
    pieces = refs[:fronts]
    halo_ref, forcing_ref, first_ref, slope_ref, field_ref, hidden_ref, ready_ref, piece = refs[fronts:]
    sizes = (fronts, pitch, hidden, cells)
    chan = lax.axis_index("chan")
    live = lax.axis_index("tm") < lax.axis_size("tm") - 1
    field_ref[...] = jnp.zeros_like(field_ref)
    for p, ref in enumerate(pieces):
        start = ((chan if p < fronts // 2 else 1 - chan) + 1) * 2 * pitch
        front = 2 * (p % (fronts // 2))
        spread_rows((states, pitch, cells), ref, front, piece, field_ref, start, live)
    for j in (2, 3):
        slope = slope_ref[j * hidden:(j + 1) * hidden, :].astype(jnp.float32)
        hidden_row(sizes, j, first_ref, slope, field_ref, hidden_ref, range(fronts // 2))
    ready_ref[...] = forcing_ref[...].astype(jnp.float32)
    for h in range(4):
        for f in range(fronts):
            before = field_ref[(h + 2) * pitch:(h + 3) * pitch, f * cells:(f + 1) * cells].astype(jnp.float32)
            spots = pl.ds(f * states * 4 + h, states, stride=4)
            ready_ref[spots, :] = ready_ref[spots, :] + before[:states]
    pair = fronts // 2 - 1
    outside = outside_grid()
    spread_rows(
        (states, pitch, cells), halo_ref, 2 * pair, piece, field_ref, chan * 6 * pitch, live & ~outside
    )
    edge = halo_ref[halo_ref.shape[0] - hidden:, :].astype(jnp.float32)
    for i in range(2):
        j = 4 * chan + i
        slope = slope_ref[pl.ds(pl.multiple_of(j * hidden, 16), hidden), :].astype(jnp.float32)
        slope = jnp.where(chan == i, jnp.where(outside, 0.0, edge), slope)
        hidden_row(sizes, j, first_ref, slope, field_ref, hidden_ref, (pair,))


def step_kernel(dims, *refs):
    fronts, states, pitch, hidden, cells = dims
    pieces = refs[:fronts]
    _, _, _, first_ref, second_ref, slope_ref = refs[fronts:fronts + 6]
    result_ref, field, hidden_grad, result, piece, sem = refs[fronts + 6:]
    edge_ref = pieces[fronts // 2 - 1]
    edge = edge_ref.shape[0] - hidden
    chan = lax.axis_index("chan")
    rows = 4
    sizes = (fronts, pitch, hidden, cells)
    live = lax.axis_index("tm") < lax.axis_size("tm") - 1
    border = outside_grid()
    for p, ref in enumerate(pieces):
        if p == fronts // 2 - 1:
            continue
        used = live & ~border if p < fronts // 2 else live
        start = (chan if p < fronts // 2 else 1 - chan) * 6 * pitch
        front = 2 * (p % (fronts // 2))
        spread_rows((states, pitch, cells), ref, front, piece, field, start, used)
    for j in (0, 1, rows, rows + 1):
        slope = slope_ref[j * hidden:(j + 1) * hidden, :].astype(jnp.float32)
        if j in (0, rows + 1):
            beyond = jnp.where(border, 0.0, edge_ref[edge:, :].astype(jnp.float32))
            slope = jnp.where(chan == (0 if j == 0 else 1), beyond, slope)
        hidden_row(sizes, j, first_ref, slope, field, hidden_grad, range(fronts // 2 - 1))
    for i in range(2):
        j = 4 * (1 - chan) + i
        slope = slope_ref[pl.ds(pl.multiple_of(j * hidden, 16), hidden), :].astype(jnp.float32)
        hidden_row(sizes, j, first_ref, slope, field, hidden_grad, (fronts // 2 - 1,))

    size = 2 * states * rows
    copies = []
    for pair in range(fronts // 2):
        part = slice(pair * size, (pair + 1) * size)
        block = slice(2 * pair * cells, 2 * (pair + 1) * cells)
        for h in range(rows):
            taps = jnp.dot(
                second_ref[...], hidden_grad[h * hidden:(h + 3) * hidden, block],
                preferred_element_type=jnp.float32,
            )
            for f in range(2):
                lanes = slice(f * cells, (f + 1) * cells)
                total = (
                    taps[pitch:2 * pitch, lanes]
                    + lane_shift(taps[0:pitch, lanes], -1)
                    + lane_shift(taps[2 * pitch:3 * pitch, lanes], 1)
                )
                spots = pl.ds((2 * pair + f) * states * rows + h, states, stride=rows)
                result[spots, :] = result[spots, :] + total[:states]
        copies.append(pltpu.make_async_copy(result.at[part], result_ref.at[part], sem.at[pair]))
        copies[-1].start()
    for copy in copies:
        copy.wait()


def per_device(innovations, obs_mask, slopes, layer_of, weight_in, weight_out):
    fronts, _, states, rows, cells = innovations.shape
    half = slopes.shape[1]
    hidden = 2 * half
    pitch = -(-states // 16) * 16
    owners = lax.axis_size("tm")
    flat = (fronts * states * rows, cells)

    def array(shape, dtype=jnp.bfloat16):
        return jax.ShapeDtypeStruct(shape, dtype)

    pairs = fronts // 2
    pieces = (array((4 * states, cells)),) * fronts
    piece_wide = pltpu.VMEM(pieces[0].shape, jnp.float32)
    join = -(-4 * states // 16) * 16
    field_shape, hidden_shape = (8 * pitch, fronts * cells), (6 * hidden, fronts * cells)
    modest = pltpu.CompilerParams(vmem_limit_bytes=8 << 20)
    *sent, forcing, raw_own = pl.pallas_call(
        functools.partial(first_kernel, (fronts, states, cells, half)),
        out_shape=pieces + (array(flat), array((26 * half, cells))),
        in_specs=[HBM] * 6,
        out_specs=(VMEM,) * (fronts + 2),
        scratch_shapes=[
            pltpu.SMEM(layer_of.shape, jnp.int32),
            pltpu.SMEM(obs_mask.shape[2:], jnp.int32),
            pltpu.VMEM(flat, jnp.bfloat16),
            pltpu.VMEM((8 * half, cells), jnp.bfloat16),
            pltpu.VMEM((3, 3, half, states), jnp.bfloat16),
            pltpu.VMEM((3, 3, half, states), jnp.bfloat16),
            pltpu.VMEM(flat, jnp.float32),
            piece_wide,
            pltpu.SemaphoreType.DMA((10,)),
        ],
        compiler_params=modest,
    )(
        *(
            pltpu.with_memory_space_constraint(argument, pltpu.HBM)
            for argument in (
                layer_of, obs_mask[0, 0], innovations.reshape(flat), slopes.reshape(8 * half, cells),
                weight_out, weight_in.transpose(0, 1, 2, 4, 3),
            )
        )
    )
    outer = [to_earlier(block) for block in sent[:pairs]]
    raw_away = swap_chan(raw_own)
    first, second, slope, edge = pl.pallas_call(
        functools.partial(order_kernel, (states, pitch, half, cells)),
        out_shape=(
            array((3 * hidden, 2 * cells)), array((3 * pitch, 3 * hidden)),
            array((6 * hidden, cells)), array((hidden, cells)),
        ),
        in_specs=[VMEM] * 2,
        out_specs=(VMEM,) * 4,
        scratch_shapes=[pltpu.VMEM((8 * half, cells), jnp.float32)],
        compiler_params=modest,
    )(raw_own, raw_away)
    inner = [to_earlier(block) for block in sent[pairs:]]

    for hop in range(1, owners):
        if hop > 1:
            sent = pl.pallas_call(
                functools.partial(split_kernel, (fronts, states, cells)),
                out_shape=pieces,
                in_specs=[VMEM],
                out_specs=(VMEM,) * fronts,
                scratch_shapes=[pltpu.VMEM(flat, jnp.float32), piece_wide],
                compiler_params=modest,
            )(result)
            outer = [to_earlier(block) for block in sent[:pairs]]
            inner = [to_earlier(block) for block in sent[pairs:]]
        joined = pl.pallas_call(
            functools.partial(join_kernel, join),
            out_shape=array((join + hidden, cells)),
            in_specs=[VMEM, VMEM],
            out_specs=VMEM,
            compiler_params=modest,
        )(outer[-1], edge)
        halo = [swap_lat(block) for block in outer[:-1] + [joined]]
        other = [swap_chan(block) for block in inner]
        sizes = (fronts, states, pitch, hidden, cells)
        own, middle, ready = pl.pallas_call(
            functools.partial(own_kernel, sizes),
            out_shape=(array(field_shape), array(hidden_shape), array(flat, jnp.float32)),
            in_specs=[VMEM] * (fronts + 4),
            out_specs=(VMEM,) * 3,
            scratch_shapes=[piece_wide],
            compiler_params=modest,
        )(*outer, *inner, halo[-1], forcing, first, slope)
        result, _, _, _ = pl.pallas_call(
            functools.partial(step_kernel, sizes),
            out_shape=(array(flat, jnp.float32), array(field_shape), array(hidden_shape), array(flat, jnp.float32)),
            in_specs=[VMEM] * (fronts + 6),
            out_specs=(HBM, VMEM, VMEM, VMEM),
            input_output_aliases={fronts: 1, fronts + 1: 2, fronts + 2: 3},
            scratch_shapes=[
                piece_wide,
                pltpu.SemaphoreType.DMA((fronts // 2,)),
            ],
            compiler_params=modest,
        )(*halo, *other, own, middle, ready, first, second, slope)
    return result.reshape(innovations.shape)


def solution(mesh):
    return jax.shard_map(
        per_device,
        mesh=mesh,
        in_specs=(
            P(None, ("grp", "tm"), None, ("lat", "chan"), None),
            P(("grp", "tm"), ("lat", "chan"), None),
            P(("grp", "tm"), "chan", "lat", None),
            P(),
            P(None, None, None, None, "chan"),
            P(None, None, None, "chan", None),
        ),
        out_specs=P(None, ("grp", "tm"), None, ("lat", "chan"), None),
        check_vma=False,
    )
```
